256 devices in a mesh: lon: 64 (over z, x, core), lat: 4 (over y).
Axes of the slice: x: 4, y: 4, z: 8, core: 2. Of those that a mesh axis runs over, the one named last changes fastest.
Arguments:
- thermal_departure: float32 [90, 128, 8192], P(None, 'lat', 'lon'), may hold values from -6 to 6
- moisture_profile: float32 [90, 128, 8192], P(None, 'lat', 'lon'), may hold values from -6 to 6
- solar_elevation_factor: float32 [128, 8192], P('lat', 'lon'), may hold values from 0.1 to 1
- daylight_groups: int32 [128, 64], P('lat', 'lon'), may hold values from 0 to 1, as said below
- spreading_factor: float32 [128, 8192], P('lat', 'lon'), may hold values from 0.03 to 0.24
- entry_layer_matrix: float32 [512, 181], replicated, may hold values from -0.4375 to 0.4375
- entry_layer_offset: float32 [512], replicated, may hold values from -3 to 3
- inner_layer_matrices: float32 [2, 512, 512], replicated, may hold values from -0.25 to 0.25
- inner_layer_offsets: float32 [2, 512], replicated, may hold values from -3 to 3
- final_layer_matrix: float32 [90, 512], replicated, may hold values from -0.25 to 0.25
- final_layer_offset: float32 [90], replicated, may hold values from -3 to 3
Outputs:
- heating: float32 [90, 128, 8192], P(None, 'lat', 'lon')
- temp_next: float32 [90, 128, 8192], P(None, 'lat', 'lon')
The draws below stay inside these ranges and needn't reach their ends.
Inputs may be any that keep to these rules, and one draw needn't show every extreme that they name: In every row the sunlit strips form one run of 32 consecutive strips, wrapping around, so daylight_groups[r, j] + daylight_groups[r, (j + 32) mod 64] == 1; row r and row r + 32 are complements of each other.
All inputs are finite; a program needn't handle non-finite values.
Results may differ from the reference program's by a relative error of at most 0.0001.
Values sent between devices are 32-bit elements; how exact they have to be, the bound alone decides.
No kernel may reach another device: no remote copies, remote signals or barrier semaphores. Data moves between devices by JAX's collectives and lax.ppermute only.
A program may use at most 64 MiB of HBM per device.

```python
import math
import jax
import jax.numpy as jnp
from jax import lax

ALTITUDE_TIERS = 90
HID = 512
DEPTH = 2
BLOCK = 128
NB = 32
STEPS = 2
FEAT = 181
MERIDIAN_SPAN = 128
ZONAL_SPAN = 8192
STRIPS = 64


def draw_daylight_groups(key, part):
    key_base = jax.random.fold_in(key, 11)
    key_jitter = jax.random.fold_in(key, 23)
    base = jax.random.randint(key_base, (), 0, STRIPS)
    jitter_local = jax.random.randint(key_jitter, (NB,), -1, 2)
    row_index = jnp.arange(MERIDIAN_SPAN, dtype=jnp.int32)
    band_flip = jnp.mod(row_index // NB, 2) * (STRIPS // 2)
    jitter = jitter_local[jnp.mod(row_index, NB)] + band_flip
    strip = jnp.arange(STRIPS, dtype=jnp.int32)
    offset = jnp.mod(strip[None, :] - base - jitter[:, None], STRIPS)
    return jnp.where(offset < STRIPS // 2, 1, 0).astype(jnp.int32)


def block_scale(key, extent, pieces, low, top_value):
    loudness = 1.0
    for position, blocks in pieces:
        steps = jax.random.uniform(jax.random.fold_in(jax.random.fold_in(key, 6), position), (blocks,), jnp.float32, low / len(pieces), top_value / len(pieces))
        loudness = loudness * jnp.repeat(jnp.exp(steps), extent[position] // blocks).reshape((-1,) + (1,) * (len(extent) - 1 - position))
    return loudness


def bell_draw(own_key, shape, spread, reach, split=(), held_as=jnp.bfloat16):
    values = spread * jax.random.normal(own_key, shape, jnp.float32)
    if split:
        values = values * block_scale(own_key, shape, split, -0.22, 0.18)
    return jnp.clip(values, -reach, reach).astype(held_as)


def setup_inputs(seed: int = 0) -> dict:
    seeds = jax.random.split(jax.random.key(seed), 12)
    return {
        "thermal_departure": bell_draw(seeds[0], (ALTITUDE_TIERS, MERIDIAN_SPAN, ZONAL_SPAN), 1.0, 6.0, ((1, 4), (2, 64)), jnp.float32),
        "moisture_profile": bell_draw(seeds[1], (ALTITUDE_TIERS, MERIDIAN_SPAN, ZONAL_SPAN), 1.0, 6.0, ((1, 4), (2, 64)), jnp.float32),
        "solar_elevation_factor": jnp.clip(0.1 + 0.9 * jax.random.uniform(seeds[2], (MERIDIAN_SPAN, ZONAL_SPAN), jnp.float32) ** block_scale(seeds[2], (MERIDIAN_SPAN, ZONAL_SPAN), ((0, 4), (1, 64)), -0.2, 0.2), 0.1, 1.0),
        "daylight_groups": draw_daylight_groups(jax.random.fold_in(seeds[11], 71), 0),
        "spreading_factor": jnp.clip(jnp.exp(math.log(0.24) - 2.0794415 * jax.random.uniform(seeds[4], (MERIDIAN_SPAN, ZONAL_SPAN), jnp.float32) ** block_scale(seeds[4], (MERIDIAN_SPAN, ZONAL_SPAN), ((0, 4), (1, 64)), -0.2, 0.2)), 0.03, 0.24),
        "entry_layer_matrix": bell_draw(seeds[5], (HID, FEAT), FEAT ** -0.5, 0.4375, (), jnp.float32),
        "entry_layer_offset": bell_draw(seeds[6], (HID,), 0.5, 3.0, (), jnp.float32),
        "inner_layer_matrices": bell_draw(seeds[7], (DEPTH, HID, HID), HID ** -0.5, 0.25, (), jnp.float32),
        "inner_layer_offsets": bell_draw(seeds[8], (DEPTH, HID), 0.5, 3.0, (), jnp.float32),
        "final_layer_matrix": bell_draw(seeds[9], (ALTITUDE_TIERS, HID), HID ** -0.5, 0.25, (), jnp.float32),
        "final_layer_offset": bell_draw(seeds[10], (ALTITUDE_TIERS,), 0.5, 3.0, (), jnp.float32),
    }


def network_apply(columns, entry_layer_matrix, entry_layer_offset, inner_layer_matrices, inner_layer_offsets, final_layer_matrix, final_layer_offset):
    hidden = jax.nn.silu(jnp.dot(entry_layer_matrix, columns, precision=lax.Precision.HIGHEST) + entry_layer_offset[:, None])
    for layer in range(DEPTH):
        hidden = jax.nn.silu(jnp.dot(inner_layer_matrices[layer], hidden, precision=lax.Precision.HIGHEST) + inner_layer_offsets[layer][:, None])
    return jnp.dot(final_layer_matrix, hidden, precision=lax.Precision.HIGHEST) + final_layer_offset[:, None]


def diffuse(atmosphere_snapshot, spreading_factor):
    padded = jnp.concatenate([atmosphere_snapshot[:, :, -1:], atmosphere_snapshot, atmosphere_snapshot[:, :, :1]], axis=2)
    padded = jnp.pad(padded, ((0, 0), (1, 1), (0, 0)))
    beside_all = padded[:, :-2, 1:-1] + padded[:, 2:, 1:-1] + padded[:, 1:-1, :-2] + padded[:, 1:-1, 2:]
    return atmosphere_snapshot + spreading_factor[None] * (beside_all - 4.0 * atmosphere_snapshot)


def reference(thermal_departure, moisture_profile, solar_elevation_factor, daylight_groups, spreading_factor, entry_layer_matrix, entry_layer_offset, inner_layer_matrices, inner_layer_offsets, final_layer_matrix, final_layer_offset):
    thermal_tracks = jnp.moveaxis(thermal_departure, 1, 0)
    moisture_tracks = jnp.moveaxis(moisture_profile, 1, 0)

    def single_parallel(packed):
        temp_row, humid_row, cos_row, lit_row = packed
        columns = jnp.concatenate([temp_row, humid_row, cos_row[None]], axis=0)
        output = network_apply(columns, entry_layer_matrix, entry_layer_offset, inner_layer_matrices, inner_layer_offsets, final_layer_matrix, final_layer_offset)
        lit_cols = jnp.repeat(lit_row.astype(jnp.float32), BLOCK)
        return output * (cos_row * lit_cols)[None]

    warming_tracks = lax.map(single_parallel, (thermal_tracks, moisture_tracks, solar_elevation_factor, daylight_groups))
    heating = jnp.moveaxis(warming_tracks, 0, 1)
    atmosphere_snapshot = thermal_departure
    for substep in range(STEPS):
        atmosphere_snapshot = diffuse(atmosphere_snapshot, spreading_factor)
    return heating, atmosphere_snapshot + heating
```

```python
import functools

import jax
import jax.numpy as jnp
from jax import lax
from jax.experimental import pallas as pl
from jax.experimental.pallas import tpu as pltpu
from jax.sharding import PartitionSpec as P

F32 = jnp.float32
BF16 = jnp.bfloat16
F8 = jnp.float8_e4m3fn

LEV = 90
PAD = 96
ROWS = 32
COLS = 128
HID = 512
FEAT = 181
KIN = 256
CHUNK = 8
GROUPS = 4
W_LO = 2.0**15
W_HI = 2.0**6
X_LO = 2.0**9

VMEM = pl.BlockSpec(memory_space=pltpu.VMEM)
SMEM = pl.BlockSpec(memory_space=pltpu.SMEM)


def split(x):
    hi = x.astype(BF16)
    return hi, (x - hi.astype(F32)).astype(BF16)


def lane_index():
    return lax.broadcasted_iota(jnp.int32, (PAD, COLS), 1)


def pack_kernel(t_ref, k_ref, up_ref, down_ref, west_ref, east_ref, row_s):
    row_s[...] = jnp.zeros_like(row_s)
    lane = lane_index()
    west = jnp.zeros((PAD, COLS), F32)
    east = jnp.zeros((PAD, COLS), F32)
    for r in range(ROWS):
        row_s[r, 0:LEV, :] = t_ref[:, r, :]
        row_s[r, LEV : LEV + 1, :] = k_ref[r : r + 1, :]
    for r in range(ROWS):
        block = row_s[r]
        place = 2 * (r + 1)
        here = (lane == place) | (lane == place + 1)
        west = jnp.where(here, pltpu.roll(block, place, 1), west)
        east = jnp.where(here, pltpu.roll(block, place + 2, 1), east)
    west_ref[...] = west
    east_ref[...] = east
    up_ref[0:PAD] = row_s[0]
    up_ref[PAD:] = row_s[1]
    down_ref[0:PAD] = row_s[ROWS - 1]
    down_ref[PAD:] = row_s[ROWS - 2]


def pack(t, k):
    edge = jax.ShapeDtypeStruct((2 * PAD, COLS), F32)
    side = jax.ShapeDtypeStruct((PAD, COLS), F32)
    return pl.pallas_call(
        pack_kernel,
        out_shape=(edge, edge, side, side),
        in_specs=[VMEM] * 2,
        out_specs=(VMEM,) * 4,
        scratch_shapes=[pltpu.VMEM((ROWS, PAD, COLS), F32)],
        compiler_params=pltpu.CompilerParams(vmem_limit_bytes=16 << 20),
        cost_estimate=pl.CostEstimate(flops=10**6, bytes_accessed=2 * 10**6, transcendentals=0),
    )(t, k)


def corner_kernel(north_ref, south_ref, west_ref, east_ref, w_out, e_out):
    lane = lane_index()
    west, east = west_ref[...], east_ref[...]
    for block, r in ((north_ref[0:PAD], -1), (south_ref[0:PAD], ROWS)):
        place = 2 * (r + 1)
        here = (lane == place) | (lane == place + 1)
        rolled = pltpu.roll(block, place, 1) if place else block
        west = jnp.where(here, rolled, west)
        east = jnp.where(here, pltpu.roll(block, place + 2, 1), east)
    w_out[...] = west
    e_out[...] = east


def corners(north, south, west, east):
    side = jax.ShapeDtypeStruct((PAD, COLS), F32)
    return pl.pallas_call(
        corner_kernel,
        out_shape=(side, side),
        in_specs=[VMEM] * 4,
        out_specs=(VMEM, VMEM),
        compiler_params=pltpu.CompilerParams(vmem_limit_bytes=8 << 20),
        cost_estimate=pl.CostEstimate(flops=10**5, bytes_accessed=4 * 10**5, transcendentals=0),
    )(north, south, west, east)


def lit_rows(lit_ref, list_s):
    for r in range(ROWS):
        list_s[r] = 0

    def step(r, carry):
        n, last = carry
        lit = lit_ref[r, 0] > 0

        @pl.when(lit)
        def _():
            list_s[n] = r

        return jnp.where(lit, n + 1, n), jnp.where(lit, r, last)

    n, last = lax.fori_loop(0, ROWS, step, (jnp.int32(0), jnp.int32(0)))

    def fill(i, _):
        list_s[i] = last
        return 0

    lax.fori_loop(n, ROWS, fill, 0)
    return n


def column_of(row, n):
    hi = row.astype(BF16)
    rest = row - hi.astype(F32)
    mid = rest.astype(BF16)
    low = (rest - mid.astype(F32)).astype(BF16)
    parts = jnp.concatenate([hi, mid, low, jnp.zeros((13, n), BF16)], axis=0)
    return lax.dot_general(
        parts, jnp.ones((16, COLS), BF16), (((0,), (0,)), ((), ())), preferred_element_type=F32
    )


def power_below(bound):
    scale = jnp.float32(1.0)
    for k in range(9):
        scale = jnp.where(bound > 440.0 * 2.0**k, scale * 0.5, scale)
    return scale


def put3(dst, w, n):
    hi, lo = split(w)
    dst[:, 0:n] = hi
    dst[:, n : 2 * n] = hi
    dst[:, 2 * n : 3 * n] = lo


def prepare(w1_ref, b1_ref, w2_ref, b2_ref, w4_ref, b4_ref, w1s, w2s, w28, w4s, bs, sc):
    w1 = w1_ref[...]
    put3(w1s, jnp.concatenate([w1 * 0.5, jnp.zeros((HID, KIN - FEAT), F32)], axis=1), KIN)
    for k in range(2):
        w = w2_ref[k] * 0.5
        hi = w.astype(BF16)
        w2s[k] = hi
        w28[k, :, 0:HID] = ((w - hi.astype(F32)) * W_LO).astype(F8)
        w28[k, :, HID : 2 * HID] = (w * W_HI).astype(F8)
    put3(w4s, jnp.concatenate([w4_ref[...], jnp.zeros((PAD - LEV, HID), F32)], axis=0), HID)
    bs[0:HID] = column_of(b1_ref[...] * 0.5, HID)
    for k in range(2):
        bs[(k + 1) * HID : (k + 2) * HID] = column_of(b2_ref[k : k + 1] * 0.5, HID)
    bs[3 * HID : 3 * HID + PAD] = jnp.concatenate(
        [column_of(b4_ref[...], LEV), jnp.zeros((PAD - LEV, COLS), F32)], axis=0
    )
    bound = 6.0 * jnp.max(jnp.sum(jnp.abs(w1), axis=1, keepdims=True)) + jnp.max(jnp.abs(b1_ref[...]))
    sc[0] = power_below(bound)
    bound = bound * jnp.max(jnp.sum(jnp.abs(w2_ref[0]), axis=1, keepdims=True)) + jnp.max(
        jnp.abs(b2_ref[...])
    )
    sc[1] = power_below(bound)


def half_silu(u):
    return u + u * jnp.tanh(u)


def dot3(w, x):
    hi, lo = split(x)
    return jnp.dot(w[...], jnp.concatenate([hi, lo, hi], axis=0), preferred_element_type=F32)


def parts8(x, scale):
    hi = x.astype(BF16)
    low = x - hi.astype(F32)
    eight = jnp.concatenate([(x * scale).astype(F8), (low * (scale * X_LO)).astype(F8)], axis=0)
    return hi, eight


def network_chunk(c, list_s, t_ref, m_ref, s_ref, w1s, w2s, w28, w4s, bs, sc, xs, put):
    rows = [list_s[c * CHUNK + j] for j in range(CHUNK)]
    n = CHUNK // GROUPS
    tile = lambda b: jnp.concatenate([b] * n, axis=1)
    scale = [sc[0], sc[1]]
    back = [1.0 / (W_LO * s) for s in scale]
    for j in range(CHUNK):
        cols = slice(j * COLS, (j + 1) * COLS)
        xs[0:LEV, cols] = t_ref[:, rows[j], :]
        xs[LEV : 2 * LEV, cols] = m_ref[:, rows[j], :]
        xs[2 * LEV : FEAT, cols] = s_ref[pl.ds(rows[j], 1), :]
    held = [None] * GROUPS
    for g in range(GROUPS):
        x = xs[:, g * n * COLS : (g + 1) * n * COLS]
        held[g] = parts8(half_silu(dot3(w1s, x) + tile(bs[0:HID])), scale[0])
    for k in range(2):
        for g in range(GROUPS):
            hi, eight = held[g]
            v = jnp.dot(w2s[k], hi, preferred_element_type=F32)
            v = v + jnp.dot(w28[k], eight, preferred_element_type=F32) * back[k]
            h = half_silu(v + tile(bs[(k + 1) * HID : (k + 2) * HID]))
            held[g] = parts8(h, scale[1]) if k == 0 else h
    for g in range(GROUPS):
        o = dot3(w4s, held[g]) + tile(bs[3 * HID : 3 * HID + PAD])
        for j in range(n):
            row = rows[g * n + j]
            put(g * n + j, row, o[:, j * COLS : (j + 1) * COLS] * s_ref[pl.ds(row, 1), :])


WEIGHTS = (
    ((HID, 3 * KIN), BF16),
    ((2, HID, HID), BF16),
    ((2, HID, 2 * HID), F8),
    ((PAD, 3 * HID), BF16),
    ((3 * HID + PAD, COLS), F32),
)
ROW_BLOCK = (CHUNK, PAD, COLS)


def first_kernel(lit, t, m, s, w1, b1, w2, b2, w4, b4, w1s, w2s, w28, w4s, bs, sc, out, list_s, xs):
    n = lit_rows(lit, list_s)

    @pl.when(n > 0)
    def _():
        prepare(w1, b1, w2, b2, w4, b4, w1s, w2s, w28, w4s, bs, sc)
        xs[176:KIN] = jnp.zeros((KIN - 176, CHUNK * COLS), F32)

        def put(j, row, value):
            out[j] = value

        network_chunk(0, list_s, t, m, s, w1s, w2s, w28, w4s, bs, sc, xs, put)


def first(lit, t, m, s, *weights):
    return pl.pallas_call(
        first_kernel,
        out_shape=tuple(jax.ShapeDtypeStruct(*w) for w in WEIGHTS)
        + (jax.ShapeDtypeStruct((2,), F32), jax.ShapeDtypeStruct(ROW_BLOCK, F32)),
        in_specs=[SMEM] + [VMEM] * 9,
        out_specs=(VMEM,) * 5 + (SMEM, VMEM),
        scratch_shapes=[pltpu.SMEM((ROWS,), jnp.int32), pltpu.VMEM((KIN, CHUNK * COLS), F32)],
        compiler_params=pltpu.CompilerParams(vmem_limit_bytes=32 << 20),
        cost_estimate=pl.CostEstimate(flops=5 * 10**9, bytes_accessed=8 * 10**6, transcendentals=0),
    )(lit, t, m, s, *weights)


def second_kernel(lit, t, m, s, w1s, w2s, w28, w4s, bs, sc, out, list_s, xs):
    n = lit_rows(lit, list_s)

    @pl.when(n > CHUNK)
    def _():
        xs[176:KIN] = jnp.zeros((KIN - 176, CHUNK * COLS), F32)

        def put(j, row, value):
            out[j] = value

        network_chunk(1, list_s, t, m, s, w1s, w2s, w28, w4s, bs, sc, xs, put)


def second(lit, t, m, s, *prepared):
    return pl.pallas_call(
        second_kernel,
        out_shape=jax.ShapeDtypeStruct(ROW_BLOCK, F32),
        in_specs=[SMEM] + [VMEM] * 8 + [SMEM],
        out_specs=VMEM,
        scratch_shapes=[pltpu.SMEM((ROWS,), jnp.int32), pltpu.VMEM((KIN, CHUNK * COLS), F32)],
        compiler_params=pltpu.CompilerParams(vmem_limit_bytes=32 << 20),
        cost_estimate=pl.CostEstimate(flops=5 * 10**9, bytes_accessed=8 * 10**6, transcendentals=0),
    )(lit, t, m, s, *prepared)


def last_kernel(
    lit, t, m, s, w1s, w2s, w28, w4s, bs, sc, heat_a, heat_b, k, north, south, mine_w, mine_e, west, east,
    heat_out, temp_out, list_s, xs, heat_s, state, step_s,
):
    n = lit_rows(lit, list_s)
    heat_s[...] = jnp.zeros_like(heat_s)

    for part, block in ((0, heat_a), (1, heat_b)):
        @pl.when(n > part * CHUNK)
        def _():
            for j in range(CHUNK):
                heat_s[list_s[part * CHUNK + j]] = block[j]

    @pl.when(n > 2 * CHUNK)
    def _():
        xs[176:KIN] = jnp.zeros((KIN - 176, CHUNK * COLS), F32)

        def put(j, row, value):
            heat_s[row] = value

        def one(c, _):
            network_chunk(c, list_s, t, m, s, w1s, w2s, w28, w4s, bs, sc, xs, put)
            return 0

        lax.fori_loop(2, (n + CHUNK - 1) // CHUNK, one, 0)

    state[0] = north[PAD:]
    state[1] = north[0:PAD]
    for r in range(ROWS):
        state[r + 2, 0:LEV, :] = t[:, r, :]
        state[r + 2, LEV : LEV + 1, :] = k[r : r + 1, :]
        state[r + 2, LEV + 1 : PAD, :] = jnp.zeros((PAD - LEV - 1, COLS), F32)
    state[ROWS + 2] = south[0:PAD]
    state[ROWS + 3] = south[PAD:]
    lane = lane_index()
    odd = lane % 2 == 1
    side = jnp.where(odd, west[...], east[...])

    def compact(far, own, towards):
        near = far[...]
        number = near[LEV : LEV + 1, :]
        around = (
            pltpu.roll(near, 2, 1)
            + pltpu.roll(near, COLS - 2, 1)
            + pltpu.roll(near, towards, 1)
            + pltpu.roll(own[...], towards, 1)
        )
        return near + number * (around - 4.0 * near)

    side_next = jnp.where(odd, compact(west, mine_w, 1), compact(east, mine_e, COLS - 1))
    first_lane, last_lane = lane == 0, lane == COLS - 1

    def substep(above, here, below, number, sides, r):
        edge = pltpu.roll(sides, (-(2 * r + 3)) % COLS, 1)
        left = jnp.where(first_lane, edge, pltpu.roll(here, 1, 1))
        right = jnp.where(last_lane, edge, pltpu.roll(here, COLS - 1, 1))
        return here + number * (above + below + left + right - 4.0 * here)

    for r in range(-1, ROWS + 1):
        number = state[r + 2, LEV : LEV + 1, :]
        step_s[r + 1] = substep(state[r + 1], state[r + 2], state[r + 3], number, side, r)
    for r in range(ROWS):
        number = state[r + 2, LEV : LEV + 1, :]
        done = substep(step_s[r], step_s[r + 1], step_s[r + 2], number, side_next, r)
        heat = heat_s[r]
        heat_out[:, r, :] = heat[0:LEV]
        temp_out[:, r, :] = (done + heat)[0:LEV]


def last(lit, t, m, s, prepared, *rest):
    whole = jax.ShapeDtypeStruct((LEV, ROWS, COLS), F32)
    return pl.pallas_call(
        last_kernel,
        out_shape=(whole, whole),
        in_specs=[SMEM] + [VMEM] * 8 + [SMEM] + [VMEM] * 9,
        out_specs=(VMEM, VMEM),
        scratch_shapes=[
            pltpu.SMEM((ROWS,), jnp.int32),
            pltpu.VMEM((KIN, CHUNK * COLS), F32),
            pltpu.VMEM((ROWS, PAD, COLS), F32),
            pltpu.VMEM((ROWS + 4, PAD, COLS), F32),
            pltpu.VMEM((ROWS + 2, PAD, COLS), F32),
        ],
        compiler_params=pltpu.CompilerParams(vmem_limit_bytes=40 << 20),
        cost_estimate=pl.CostEstimate(flops=10**10, bytes_accessed=8 * 10**6, transcendentals=0),
    )(lit, t, m, s, *prepared, *rest)


def on_device(t, m, s, lit, k, w1, b1, w2, b2, w4, b4):
    lats, lons = lax.axis_size("lat"), lax.axis_size("lon")
    up, down, west, east = pack(t, k)
    north = lax.ppermute(down, "lat", [(i, i + 1) for i in range(lats - 1)])
    south = lax.ppermute(up, "lat", [(i + 1, i) for i in range(lats - 1)])
    *prepared, heat_a = first(lit, t, m, s, w1, b1.reshape(1, HID), w2, b2, w4, b4.reshape(1, LEV))
    west, east = corners(north, south, west, east)
    from_east = lax.ppermute(west, "lon", [(i, (i - 1) % lons) for i in range(lons)])
    from_west = lax.ppermute(east, "lon", [(i, (i + 1) % lons) for i in range(lons)])
    heat_b = second(lit, t, m, s, *prepared)
    return last(lit, t, m, s, prepared, heat_a, heat_b, k, north, south, west, east, from_west, from_east)


def solution(mesh):
    whole, plane = P(None, "lat", "lon"), P("lat", "lon")
    return jax.shard_map(
        on_device,
        mesh=mesh,
        in_specs=(whole, whole, plane, plane, plane) + (P(),) * 6,
        out_specs=(whole, whole),
        check_vma=False,
    )
```

```python
import functools

import jax
import jax.numpy as jnp
from jax import lax
from jax.experimental import pallas as pl
from jax.experimental.pallas import tpu as pltpu
from jax.sharding import PartitionSpec as P

F32 = jnp.float32
BF16 = jnp.bfloat16
F8 = jnp.float8_e4m3fn

LEV = 90
PAD = 96
ROWS = 32
COLS = 128
HID = 512
FEAT = 181
KIN = 2 * PAD
CHUNK = 8
GROUPS = 4
W_LO = 2.0**15
W_HI = 2.0**6
X_LO = 2.0**9
LOAD_LIMIT = 32 << 20

VMEM = pl.BlockSpec(memory_space=pltpu.VMEM)
SMEM = pl.BlockSpec(memory_space=pltpu.SMEM)
HBM = pl.BlockSpec(memory_space=pltpu.HBM)


def split(x):
    hi = x.astype(BF16)
    return hi, (x - hi.astype(F32)).astype(BF16)


def lane_index():
    return lax.broadcasted_iota(jnp.int32, (PAD, COLS), 1)


def put_split(hi_ref, eight_ref, w, n):
    hi = w.astype(BF16)
    hi_ref[...] = hi
    eight_ref[:, 0:n] = ((w - hi.astype(F32)) * W_LO).astype(F8)
    eight_ref[:, n : 2 * n] = (w * W_HI).astype(F8)


def column_of(row, n):
    hi = row.astype(BF16)
    rest = row - hi.astype(F32)
    mid = rest.astype(BF16)
    low = (rest - mid.astype(F32)).astype(BF16)
    parts = jnp.concatenate([hi, mid, low, jnp.zeros((13, n), BF16)], axis=0)
    return lax.dot_general(
        parts, jnp.ones((16, COLS), BF16), (((0,), (0,)), ((), ())), preferred_element_type=F32
    )


def power_below(bound):
    scale = jnp.float32(1.0)
    for k in range(9):
        scale = jnp.where(bound > 440.0 * 2.0**k, scale * 0.5, scale)
    return scale


def put3(dst, w, n):
    hi, lo = split(w)
    dst[:, 0:n] = hi
    dst[:, n : 2 * n] = hi
    dst[:, 2 * n : 3 * n] = lo


def prepare(w1t, b1, w2, b2, w4, b4, w1s, w18, w2s, w28, w4s, bs, sc):
    gap = jnp.zeros((PAD - LEV, HID), F32)
    w1 = jnp.concatenate(
        [w1t[0:LEV], gap, w1t[LEV:FEAT], b1[...], gap[0 : PAD - LEV - 2]], axis=0
    )
    put_split(w1s, w18, jnp.transpose(w1 * 0.5), KIN)
    for k in range(2):
        put_split(w2s.at[k], w28.at[k], w2[k] * 0.5, HID)
    put3(w4s, jnp.concatenate([w4[...], gap], axis=0), HID)
    for k in range(2):
        bs[k * HID : (k + 1) * HID] = column_of(b2[k : k + 1] * 0.5, HID)
    bs[2 * HID : 2 * HID + PAD] = jnp.concatenate(
        [column_of(b4[...], LEV), jnp.zeros((PAD - LEV, COLS), F32)], axis=0
    )
    bound = 6.0 * jnp.max(jnp.sum(jnp.abs(w1), axis=0, keepdims=True))
    sc[0] = power_below(bound)
    bound = bound * jnp.max(jnp.sum(jnp.abs(w2[0]), axis=1, keepdims=True)) + jnp.max(jnp.abs(b2[...]))
    sc[1] = power_below(bound)


def first_columns(block, r, west, east):
    lane = lane_index()
    place = 2 * (r + 1)
    here = (lane == place) | (lane == place + 1)
    rolled = pltpu.roll(block, place, 1) if place else block
    return jnp.where(here, rolled, west), jnp.where(here, pltpu.roll(block, place + 2, 1), east)


def load_kernel(
    t_hbm, m_hbm, s_hbm, k_hbm, w1_hbm, b1_hbm, w2_hbm, b2_hbm, w4_hbm, b4_hbm,
    t, m, w1s, w18, w2s, w28, w4s, bs, sc, up, down, west_out, east_out,
    k, s, w1, b1, w2, b2, w4, b4, sems,
):
    state = [pltpu.make_async_copy(k_hbm, k, sems.at[0])] + [
        pltpu.make_async_copy(t_hbm.at[:, r, :], t.at[r, pl.ds(0, LEV), :], sems.at[0]) for r in range(ROWS)
    ]
    pairs = ((w1_hbm, w1), (b1_hbm, b1), (w2_hbm, w2), (b2_hbm, b2), (w4_hbm, w4), (b4_hbm, b4))
    weights = [pltpu.make_async_copy(a, b, sems.at[1]) for a, b in pairs]
    humid = [pltpu.make_async_copy(s_hbm, s, sems.at[2])] + [
        pltpu.make_async_copy(m_hbm.at[:, r, :], m.at[r, pl.ds(0, LEV), :], sems.at[2]) for r in range(ROWS)
    ]
    for copy in state + weights + humid:
        copy.start()
    for copy in state:
        copy.wait()
    blank = jnp.zeros((PAD - LEV - 1, COLS), F32)
    west = jnp.zeros((PAD, COLS), F32)
    east = jnp.zeros((PAD, COLS), F32)
    for r in range(ROWS):
        t[r, LEV:PAD, :] = jnp.concatenate([k[r : r + 1, :], blank], axis=0)
        west, east = first_columns(t[r], r, west, east)
    west_out[...] = west
    east_out[...] = east
    up[0:PAD] = t[0]
    up[PAD:] = t[1]
    down[0:PAD] = t[ROWS - 1]
    down[PAD:] = t[ROWS - 2]
    for copy in weights:
        copy.wait()
    prepare(w1, b1, w2, b2, w4, b4, w1s, w18, w2s, w28, w4s, bs, sc)
    for copy in humid:
        copy.wait()
    one = jnp.ones((1, COLS), F32)
    for r in range(ROWS):
        m[r, LEV:PAD, :] = jnp.concatenate([s[r : r + 1, :], one, blank[1:]], axis=0)


TRACK = jax.ShapeDtypeStruct((ROWS, PAD, COLS), F32)
EDGE = jax.ShapeDtypeStruct((2 * PAD, COLS), F32)
SIDE = jax.ShapeDtypeStruct((PAD, COLS), F32)
WEIGHTS = (
    ((HID, KIN), BF16),
    ((HID, 2 * KIN), F8),
    ((2, HID, HID), BF16),
    ((2, HID, 2 * HID), F8),
    ((PAD, 3 * HID), BF16),
    ((2 * HID + PAD, COLS), F32),
)


def load(t, m, s, k, w1, b1, w2, b2, w4, b4):
    return pl.pallas_call(
        load_kernel,
        out_shape=(TRACK, TRACK)
        + tuple(jax.ShapeDtypeStruct(*w) for w in WEIGHTS)
        + (jax.ShapeDtypeStruct((2,), F32), EDGE, EDGE, SIDE, SIDE),
        in_specs=[HBM] * 10,
        out_specs=(VMEM,) * 8 + (SMEM,) + (VMEM,) * 4,
        scratch_shapes=[
            pltpu.VMEM((ROWS, COLS), F32),
            pltpu.VMEM((ROWS, COLS), F32),
            pltpu.VMEM((FEAT, HID), F32),
            pltpu.VMEM((1, HID), F32),
            pltpu.VMEM((2, HID, HID), F32),
            pltpu.VMEM((2, HID), F32),
            pltpu.VMEM((LEV, HID), F32),
            pltpu.VMEM((1, LEV), F32),
            pltpu.SemaphoreType.DMA((3,)),
        ],
        compiler_params=pltpu.CompilerParams(vmem_limit_bytes=LOAD_LIMIT),
        cost_estimate=pl.CostEstimate(flops=10**6, bytes_accessed=8 * 10**6, transcendentals=0),
    )(*(pltpu.with_memory_space_constraint(x, pltpu.HBM) for x in (t, m, s, k, w1, b1, w2, b2, w4, b4)))


def corner_kernel(north_ref, south_ref, west_ref, east_ref, w_out, e_out):
    west, east = west_ref[...], east_ref[...]
    west, east = first_columns(north_ref[0:PAD], -1, west, east)
    west, east = first_columns(south_ref[0:PAD], ROWS, west, east)
    w_out[...] = west
    e_out[...] = east


def corners(north, south, west, east):
    side = jax.ShapeDtypeStruct((PAD, COLS), F32)
    return pl.pallas_call(
        corner_kernel,
        out_shape=(side, side),
        in_specs=[VMEM] * 4,
        out_specs=(VMEM, VMEM),
        compiler_params=pltpu.CompilerParams(vmem_limit_bytes=8 << 20),
        cost_estimate=pl.CostEstimate(flops=10**5, bytes_accessed=4 * 10**5, transcendentals=0),
    )(north, south, west, east)


def lit_rows(lit_ref, list_s):
    for r in range(ROWS):
        list_s[r] = 0

    def step(r, carry):
        n, last = carry
        lit = lit_ref[r] > 0

        @pl.when(lit)
        def _():
            list_s[n] = r

        return jnp.where(lit, n + 1, n), jnp.where(lit, r, last)

    n, last = lax.fori_loop(0, ROWS, step, (jnp.int32(0), jnp.int32(0)))

    def fill(i, _):
        list_s[i] = last
        return 0

    lax.fori_loop(n, ROWS, fill, 0)
    return n


def half_silu(u):
    return u + u * jnp.tanh(u)


def dot3(w, x):
    hi, lo = split(x)
    return jnp.dot(w[...], jnp.concatenate([hi, lo, hi], axis=0), preferred_element_type=F32)


def parts8(x, scale):
    hi = x.astype(BF16)
    low = x - hi.astype(F32)
    scaled = x if scale is None else x * scale
    factor = X_LO if scale is None else scale * X_LO
    return hi, jnp.concatenate([scaled.astype(F8), (low * factor).astype(F8)], axis=0)


def dot8(w, w8, held, back):
    hi, eight = held
    v = jnp.dot(w, hi, preferred_element_type=F32)
    return v + jnp.dot(w8, eight, preferred_element_type=F32) * back


def network_chunk(c, list_s, t, m, w1s, w18, w2s, w28, w4s, bs, sc, put):
    rows = [list_s[c * CHUNK + j] for j in range(CHUNK)]
    n = CHUNK // GROUPS
    tile = lambda b: jnp.concatenate([b] * n, axis=1)
    scale = [sc[0], sc[1]]
    back = [1.0 / (W_LO * s) for s in scale]
    held = [None] * GROUPS
    for g in range(GROUPS):
        x = jnp.concatenate(
            [jnp.concatenate([t[r], m[r]], axis=0) for r in rows[g * n : (g + 1) * n]], axis=1
        )
        v = dot8(w1s[...], w18[...], parts8(x, None), 1.0 / W_LO)
        held[g] = parts8(half_silu(v), scale[0])
    for k in range(2):
        for g in range(GROUPS):
            v = dot8(w2s[k], w28[k], held[g], back[k])
            h = half_silu(v + tile(bs[k * HID : (k + 1) * HID]))
            held[g] = parts8(h, scale[1]) if k == 0 else h
    for g in range(GROUPS):
        o = dot3(w4s, held[g]) + tile(bs[2 * HID : 2 * HID + PAD])
        for j in range(n):
            row = rows[g * n + j]
            put(g * n + j, row, o[:, j * COLS : (j + 1) * COLS] * m[row, LEV : LEV + 1, :])


ROW_BLOCK = jax.ShapeDtypeStruct((CHUNK, PAD, COLS), F32)


def some_rows_kernel(c, lit, t, m, w1s, w18, w2s, w28, w4s, bs, sc, out, list_s):
    n = lit_rows(lit, list_s)

    @pl.when(n > c * CHUNK)
    def _():
        def put(j, row, value):
            out[j] = value

        network_chunk(c, list_s, t, m, w1s, w18, w2s, w28, w4s, bs, sc, put)


def some_rows(c, lit, *arrays):
    return pl.pallas_call(
        functools.partial(some_rows_kernel, c),
        out_shape=ROW_BLOCK,
        in_specs=[SMEM] + [VMEM] * 8 + [SMEM],
        out_specs=VMEM,
        scratch_shapes=[pltpu.SMEM((ROWS,), jnp.int32)],
        compiler_params=pltpu.CompilerParams(vmem_limit_bytes=32 << 20),
        cost_estimate=pl.CostEstimate(flops=5 * 10**9, bytes_accessed=8 * 10**6, transcendentals=0),
    )(lit, *arrays)


def last_kernel(
    lit, t, m, w1s, w18, w2s, w28, w4s, bs, sc, heat_a, heat_b, north, south, mine_w, mine_e, west, east,
    heat_hbm, temp_hbm, list_s, heat_s, step_s, temp_s, sems,
):
    n = lit_rows(lit, list_s)

    @pl.when(n < ROWS)
    def _():
        heat_s[...] = jnp.zeros_like(heat_s)

    for part, block in ((0, heat_a), (1, heat_b)):
        @pl.when(n > part * CHUNK)
        def _():
            for j in range(CHUNK):
                heat_s[list_s[part * CHUNK + j]] = block[j]

    def put(j, row, value):
        heat_s[row] = value

    def one(c, _):
        network_chunk(c, list_s, t, m, w1s, w18, w2s, w28, w4s, bs, sc, put)
        return 0

    lax.fori_loop(2, (n + CHUNK - 1) // CHUNK, one, 0)

    def out(src, dst, r, sem):
        return pltpu.make_async_copy(src.at[r, pl.ds(0, LEV), :], dst.at[:, r, :], sem)

    for r in range(ROWS):
        out(heat_s, heat_hbm, r, sems.at[0]).start()

    def state(r):
        if r < 0:
            return north[0:PAD] if r == -1 else north[PAD:]
        if r >= ROWS:
            return south[0:PAD] if r == ROWS else south[PAD:]
        return t[r]

    def number(r):
        if r < 0:
            return north[LEV : LEV + 1]
        if r >= ROWS:
            return south[LEV : LEV + 1]
        return t[r, LEV : LEV + 1, :]

    lane = lane_index()
    odd = lane % 2 == 1
    side = jnp.where(odd, west[...], east[...])

    def compact(far, own, towards):
        near = far[...]
        number = near[LEV : LEV + 1, :]
        around = (
            pltpu.roll(near, 2, 1)
            + pltpu.roll(near, COLS - 2, 1)
            + pltpu.roll(near, towards, 1)
            + pltpu.roll(own[...], towards, 1)
        )
        return near + number * (around - 4.0 * near)

    side_next = jnp.where(odd, compact(west, mine_w, 1), compact(east, mine_e, COLS - 1))
    first_lane, last_lane = lane == 0, lane == COLS - 1

    def substep(above, here, below, number, sides, r):
        edge = pltpu.roll(sides, (-(2 * r + 3)) % COLS, 1)
        left = jnp.where(first_lane, edge, pltpu.roll(here, 1, 1))
        right = jnp.where(last_lane, edge, pltpu.roll(here, COLS - 1, 1))
        return here + number * (above + below + left + right - 4.0 * here)

    for r in range(-1, ROWS + 1):
        step_s[r + 1] = substep(state(r - 1), state(r), state(r + 1), number(r), side, r)
        if r >= 1:
            q = r - 1
            done = substep(step_s[q], step_s[q + 1], step_s[q + 2], number(q), side_next, q)
            temp_s[q] = done + heat_s[q]
            out(temp_s, temp_hbm, q, sems.at[1]).start()
    for r in range(ROWS):
        out(heat_s, heat_hbm, r, sems.at[0]).wait()
    for r in range(ROWS):
        out(temp_s, temp_hbm, r, sems.at[1]).wait()


def last(lit, *arrays):
    whole = jax.ShapeDtypeStruct((LEV, ROWS, COLS), F32)
    track = pltpu.VMEM((ROWS, PAD, COLS), F32)
    return pl.pallas_call(
        last_kernel,
        out_shape=(whole, whole),
        in_specs=[SMEM] + [VMEM] * 8 + [SMEM] + [VMEM] * 8,
        out_specs=(HBM, HBM),
        scratch_shapes=[
            pltpu.SMEM((ROWS,), jnp.int32),
            track,
            pltpu.VMEM((ROWS + 2, PAD, COLS), F32),
            track,
            pltpu.SemaphoreType.DMA((2,)),
        ],
        compiler_params=pltpu.CompilerParams(vmem_limit_bytes=32 << 20),
        cost_estimate=pl.CostEstimate(flops=10**10, bytes_accessed=8 * 10**6, transcendentals=0),
    )(lit, *arrays)


def on_device(t, m, s, lit, k, w1, b1, w2, b2, w4, b4):
    lats, lons = lax.axis_size("lat"), lax.axis_size("lon")
    lit = lit[:, 0]
    t, m, *net, up, down, west, east = load(
        t, m, s, k, w1.T, b1.reshape(1, HID), w2, b2, w4, b4.reshape(1, LEV)
    )
    north = lax.ppermute(down, "lat", [(i, i + 1) for i in range(lats - 1)])
    south = lax.ppermute(up, "lat", [(i + 1, i) for i in range(lats - 1)])
    heat_a = some_rows(0, lit, t, m, *net)
    west, east = corners(north, south, west, east)
    from_east = lax.ppermute(west, "lon", [(i, (i - 1) % lons) for i in range(lons)])
    from_west = lax.ppermute(east, "lon", [(i, (i + 1) % lons) for i in range(lons)])
    heat_b = some_rows(1, lit, t, m, *net)
    return last(lit, t, m, *net, heat_a, heat_b, north, south, west, east, from_west, from_east)


def solution(mesh):
    whole, plane = P(None, "lat", "lon"), P("lat", "lon")
    return jax.shard_map(
        on_device,
        mesh=mesh,
        in_specs=(whole, whole, plane, plane, plane) + (P(),) * 6,
        out_specs=(whole, whole),
        check_vma=False,
    )
```

```python
import functools

import jax
import jax.numpy as jnp
from jax import lax
from jax.experimental import pallas as pl
from jax.experimental.pallas import tpu as pltpu
from jax.sharding import PartitionSpec as P

F32 = jnp.float32
BF16 = jnp.bfloat16
F8 = jnp.float8_e4m3fn

LEV = 90
PAD = 96
ROWS = 32
COLS = 128
HID = 512
FEAT = 181
KIN = 2 * PAD
CHUNK = 8
GROUPS = 4
W_LO = 2.0**15
W_HI = 2.0**6
X_LO = 2.0**9
LOAD_LIMIT = 32 << 20

VMEM = pl.BlockSpec(memory_space=pltpu.VMEM)
HBM = pl.BlockSpec(memory_space=pltpu.HBM)


def split(x):
    hi = x.astype(BF16)
    return hi, (x - hi.astype(F32)).astype(BF16)


def lane_index():
    return lax.broadcasted_iota(jnp.int32, (PAD, COLS), 1)


def put_split(hi_ref, eight_ref, w, n):
    hi = w.astype(BF16)
    hi_ref[...] = hi
    eight_ref[:, 0:n] = ((w - hi.astype(F32)) * W_LO).astype(F8)
    eight_ref[:, n : 2 * n] = (w * W_HI).astype(F8)


def column_of(row, n):
    hi = row.astype(BF16)
    rest = row - hi.astype(F32)
    mid = rest.astype(BF16)
    low = (rest - mid.astype(F32)).astype(BF16)
    parts = jnp.concatenate([hi, mid, low, jnp.zeros((13, n), BF16)], axis=0)
    return lax.dot_general(
        parts, jnp.ones((16, COLS), BF16), (((0,), (0,)), ((), ())), preferred_element_type=F32
    )


def power_below(bound):
    scale = jnp.float32(1.0)
    for k in range(9):
        scale = jnp.where(bound > 440.0 * 2.0**k, 0.5 ** (k + 1), scale)
    return scale


def prepare_outer(w1t, b1, b2, w4, b4, w1s, w18, w4s, bs, sc):
    gap = jnp.zeros((PAD - LEV, HID), F32)
    w1 = jnp.concatenate(
        [w1t[0:LEV], gap, w1t[LEV:FEAT], b1[...], gap[0 : PAD - LEV - 2]], axis=0
    )
    put_split(w1s, w18, jnp.transpose(w1 * 0.5), KIN)
    hi, lo = split(jnp.concatenate([w4[...], gap], axis=0))
    w4s[0:PAD] = hi
    w4s[PAD:] = lo
    for k in range(2):
        bs[k * HID : (k + 1) * HID] = column_of(b2[k : k + 1] * 0.5, HID)
    bs[2 * HID : 2 * HID + PAD] = jnp.concatenate(
        [column_of(b4[...], LEV), jnp.zeros((PAD - LEV, COLS), F32)], axis=0
    )
    bound = 6.0 * jnp.max(jnp.sum(jnp.abs(w1), axis=0, keepdims=True))
    put_scale(sc, 0, bound)
    return bound


def put_scale(sc, k, bound):
    scale = power_below(bound)
    sc[k : k + 1] = jnp.full((1, COLS), scale)
    sc[k + 2 : k + 3] = jnp.full((1, COLS), 1.0 / (W_LO * scale))


def prepare_inner(k, w2, w2s, w28):
    put_split(w2s.at[k], w28.at[k], w2[k] * 0.5, HID)


def first_columns(block, r, west, east):
    lane = lane_index()
    place = 2 * (r + 1)
    here = (lane == place) | (lane == place + 1)
    rolled = pltpu.roll(block, place, 1) if place else block
    return jnp.where(here, rolled, west), jnp.where(here, pltpu.roll(block, place + 2, 1), east)


def load_kernel(
    t_hbm, m_hbm, s_hbm, k_hbm, w1_hbm, b1_hbm, w2_hbm, b2_hbm, w4_hbm, b4_hbm,
    t, m, w1s, w18, w2s, w28, w4s, bs, sc, up, down, west_out, east_out,
    k, s, w1, b1, w2, b2, w4, b4, sems,
):
    def rows(src, dst, sem):
        return [pltpu.make_async_copy(src.at[:, r, :], dst.at[r, pl.ds(0, LEV), :], sem) for r in range(ROWS)]

    pairs = ((w1_hbm, w1), (b1_hbm, b1), (b2_hbm, b2), (w4_hbm, w4), (b4_hbm, b4))
    outer = [pltpu.make_async_copy(a, b, sems.at[0]) for a, b in pairs]
    state = [pltpu.make_async_copy(k_hbm, k, sems.at[1])] + rows(t_hbm, t, sems.at[1])
    inner = [pltpu.make_async_copy(w2_hbm.at[i], w2.at[i], sems.at[2 + i]) for i in range(2)]
    humid = [pltpu.make_async_copy(s_hbm, s, sems.at[4])] + rows(m_hbm, m, sems.at[4])
    for copy in outer + state + inner + humid:
        copy.start()
    for copy in outer:
        copy.wait()
    bound = prepare_outer(w1, b1, b2, w4, b4, w1s, w18, w4s, bs, sc)
    for copy in state:
        copy.wait()
    blank = jnp.zeros((PAD - LEV - 1, COLS), F32)
    west = jnp.zeros((PAD, COLS), F32)
    east = jnp.zeros((PAD, COLS), F32)
    for r in range(ROWS):
        t[r, LEV:PAD, :] = jnp.concatenate([k[r : r + 1, :], blank], axis=0)
        west, east = first_columns(t[r], r, west, east)
    west_out[...] = west
    east_out[...] = east
    up[0:PAD] = t[0]
    up[PAD:] = t[1]
    down[0:PAD] = t[ROWS - 1]
    down[PAD:] = t[ROWS - 2]
    inner[0].wait()
    prepare_inner(0, w2, w2s, w28)
    bound = bound * jnp.max(jnp.sum(jnp.abs(w2[0]), axis=1, keepdims=True)) + jnp.max(jnp.abs(b2[...]))
    put_scale(sc, 1, bound)
    inner[1].wait()
    prepare_inner(1, w2, w2s, w28)
    for copy in humid:
        copy.wait()
    one = jnp.ones((1, COLS), F32)
    for r in range(ROWS):
        m[r, LEV:PAD, :] = jnp.concatenate([s[r : r + 1, :], one, blank[1:]], axis=0)


TRACK = jax.ShapeDtypeStruct((ROWS, PAD, COLS), F32)
EDGE = jax.ShapeDtypeStruct((2 * PAD, COLS), F32)
SIDE = jax.ShapeDtypeStruct((PAD, COLS), F32)
WEIGHTS = (
    ((HID, KIN), BF16),
    ((HID, 2 * KIN), F8),
    ((2, HID, HID), BF16),
    ((2, HID, 2 * HID), F8),
    ((2 * PAD, HID), BF16),
    ((2 * HID + PAD, COLS), F32),
    ((8, COLS), F32),
)


def load(*arrays):
    return pl.pallas_call(
        load_kernel,
        out_shape=(TRACK, TRACK)
        + tuple(jax.ShapeDtypeStruct(*w) for w in WEIGHTS)
        + (EDGE, EDGE, SIDE, SIDE),
        in_specs=[HBM] * 10,
        out_specs=(VMEM,) * 13,
        scratch_shapes=[
            pltpu.VMEM((ROWS, COLS), F32),
            pltpu.VMEM((ROWS, COLS), F32),
            pltpu.VMEM((FEAT, HID), F32),
            pltpu.VMEM((1, HID), F32),
            pltpu.VMEM((2, HID, HID), F32),
            pltpu.VMEM((2, HID), F32),
            pltpu.VMEM((LEV, HID), F32),
            pltpu.VMEM((1, LEV), F32),
            pltpu.SemaphoreType.DMA((5,)),
        ],
        compiler_params=pltpu.CompilerParams(vmem_limit_bytes=LOAD_LIMIT),
        cost_estimate=pl.CostEstimate(flops=10**6, bytes_accessed=8 * 10**6, transcendentals=0),
    )(*(pltpu.with_memory_space_constraint(x, pltpu.HBM) for x in arrays))


def corner_kernel(north_ref, south_ref, west_ref, east_ref, w_out, e_out):
    west, east = west_ref[...], east_ref[...]
    west, east = first_columns(north_ref[0:PAD], -1, west, east)
    west, east = first_columns(south_ref[0:PAD], ROWS, west, east)
    w_out[...] = west
    e_out[...] = east


def corners(north, south, west, east):
    side = jax.ShapeDtypeStruct((PAD, COLS), F32)
    return pl.pallas_call(
        corner_kernel,
        out_shape=(side, side),
        in_specs=[VMEM] * 4,
        out_specs=(VMEM, VMEM),
        compiler_params=pltpu.CompilerParams(vmem_limit_bytes=8 << 20),
        cost_estimate=pl.CostEstimate(flops=10**5, bytes_accessed=4 * 10**5, transcendentals=0),
    )(north, south, west, east)


def all_lit(lit_row):
    return jnp.min(lit_row[...].astype(F32)) > 0.5


def lit_rows(lit_ref, info):
    for r in range(ROWS):
        info[r] = 0

    def step(r, carry):
        n, last = carry
        lit = lit_ref[0, r] > 0

        @pl.when(lit)
        def _():
            info[n] = r

        return jnp.where(lit, n + 1, n), jnp.where(lit, r, last)

    n, last = lax.fori_loop(0, ROWS, step, (jnp.int32(0), jnp.int32(0)))

    def fill(i, _):
        info[i] = last
        return 0

    lax.fori_loop(n, ROWS, fill, 0)
    info[ROWS] = n


def count_lit(lit_row, lit_s, info, sem):
    copy = pltpu.make_async_copy(lit_row, lit_s, sem)
    copy.start()
    copy.wait()
    lit_rows(lit_s, info)
    return info[ROWS]


LIST_SCRATCH = [
    pltpu.SMEM((1, COLS), jnp.int32),
    pltpu.SMEM((ROWS + 8,), jnp.int32),
    pltpu.SemaphoreType.DMA,
]


def half_silu(u):
    return u + u * jnp.tanh(u)


def out_layer(w4s, x):
    hi, lo = split(x)
    both = jnp.dot(w4s[...], hi, preferred_element_type=F32)
    return both[0:PAD] + both[PAD:] + jnp.dot(w4s[0:PAD], lo, preferred_element_type=F32)


def parts8(x, scale):
    hi = x.astype(BF16)
    low = x - hi.astype(F32)
    scaled = x if scale is None else x * scale
    factor = X_LO if scale is None else scale * X_LO
    return hi, jnp.concatenate([scaled.astype(F8), (low * factor).astype(F8)], axis=0)


def dot8(w, w8, held, back):
    hi, eight = held
    v = jnp.dot(w, hi, preferred_element_type=F32)
    return v + jnp.dot(w8, eight, preferred_element_type=F32) * back


def network_chunk(rows, t, m, w1s, w18, w2s, w28, w4s, bs, sc, put, between=lambda: None):
    n = CHUNK // GROUPS
    tile = lambda b: jnp.concatenate([b] * n, axis=1)
    scale = [tile(sc[k : k + 1]) for k in range(2)]
    back = [tile(sc[k : k + 1]) for k in range(2, 4)]
    held = [None] * GROUPS
    for g in range(GROUPS):
        x = jnp.concatenate(
            [jnp.concatenate([t[r], m[r]], axis=0) for r in rows[g * n : (g + 1) * n]], axis=1
        )
        v = dot8(w1s[...], w18[...], parts8(x, None), 1.0 / W_LO)
        held[g] = parts8(half_silu(v), scale[0])
        between()
    for k in range(2):
        for g in range(GROUPS):
            v = dot8(w2s[k], w28[k], held[g], back[k])
            h = half_silu(v + tile(bs[k * HID : (k + 1) * HID]))
            held[g] = parts8(h, scale[1]) if k == 0 else h
            between()
    for g in range(GROUPS):
        o = out_layer(w4s, held[g]) + tile(bs[2 * HID : 2 * HID + PAD])
        for j in range(n):
            row = rows[g * n + j]
            put(g * n + j, row, o[:, j * COLS : (j + 1) * COLS] * m[row, LEV : LEV + 1, :])
        between()


def listed(info, c):
    return [info[c * CHUNK + j] for j in range(CHUNK)]


ROW_BLOCK = jax.ShapeDtypeStruct((CHUNK, PAD, COLS), F32)


def some_rows_kernel(c, lit_row, t, m, w1s, w18, w2s, w28, w4s, bs, sc, out, lit_s, info, sem):
    net = (t, m, w1s, w18, w2s, w28, w4s, bs, sc)
    every = all_lit(lit_row)

    def put(j, row, value):
        out[j] = value

    @pl.when(every)
    def _():
        network_chunk(list(range(c * CHUNK, (c + 1) * CHUNK)), *net, put)

    @pl.when(jnp.logical_not(every))
    def _():
        n = count_lit(lit_row, lit_s, info, sem)

        @pl.when(n > c * CHUNK)
        def _():
            network_chunk(listed(info, c), *net, put)


def some_rows(c, *arrays):
    return pl.pallas_call(
        functools.partial(some_rows_kernel, c),
        out_shape=ROW_BLOCK,
        in_specs=[VMEM] * 10,
        out_specs=VMEM,
        scratch_shapes=LIST_SCRATCH,
        compiler_params=pltpu.CompilerParams(vmem_limit_bytes=32 << 20),
        cost_estimate=pl.CostEstimate(flops=5 * 10**9, bytes_accessed=8 * 10**6, transcendentals=0),
    )(*arrays)


def last_kernel(
    lit_row, t, m, w1s, w18, w2s, w28, w4s, bs, sc, heat_a, heat_b, north, south, mine_w, mine_e, west, east,
    heat_hbm, temp_hbm, lit_s, info, list_sem, heat_s, step_s, temp_s, sems,
):
    net = (t, m, w1s, w18, w2s, w28, w4s, bs, sc)
    every = all_lit(lit_row)

    def heat_out(r, src=None, at=None):
        src, at = (heat_s, r) if src is None else (src, at)
        return pltpu.make_async_copy(src.at[at, pl.ds(0, LEV), :], heat_hbm.at[:, r, :], sems.at[0])

    def temp_out(r):
        return pltpu.make_async_copy(temp_s.at[r, pl.ds(0, LEV), :], temp_hbm.at[:, r, :], sems.at[1])

    def put(j, row, value):
        heat_s[row] = value

    def state(r):
        if r < 0:
            return north[0:PAD] if r == -1 else north[PAD:]
        if r >= ROWS:
            return south[0:PAD] if r == ROWS else south[PAD:]
        return t[r]

    def number(r):
        if r < 0:
            return north[LEV : LEV + 1]
        if r >= ROWS:
            return south[LEV : LEV + 1]
        return t[r, LEV : LEV + 1, :]

    lane = lane_index()
    odd = lane % 2 == 1
    side = jnp.where(odd, west[...], east[...])

    def compact(far, own, towards):
        near = far[...]
        number = near[LEV : LEV + 1, :]
        around = (
            pltpu.roll(near, 2, 1)
            + pltpu.roll(near, COLS - 2, 1)
            + pltpu.roll(near, towards, 1)
            + pltpu.roll(own[...], towards, 1)
        )
        return near + number * (around - 4.0 * near)

    side_next = jnp.where(odd, compact(west, mine_w, 1), compact(east, mine_e, COLS - 1))
    first_lane, last_lane = lane == 0, lane == COLS - 1

    def substep(above, here, below, number, sides, r):
        edge = pltpu.roll(sides, (-(2 * r + 3)) % COLS, 1)
        left = jnp.where(first_lane, edge, pltpu.roll(here, 1, 1))
        right = jnp.where(last_lane, edge, pltpu.roll(here, COLS - 1, 1))
        return here + number * (above + below + left + right - 4.0 * here)

    def step_one(r):
        step_s[r + 1] = substep(state(r - 1), state(r), state(r + 1), number(r), side, r)

    def step_two(r, heat):
        done = substep(step_s[r], step_s[r + 1], step_s[r + 2], number(r), side_next, r)
        temp_s[r] = done + heat
        temp_out(r).start()

    @pl.when(every)
    def _():
        blocks = (heat_a, heat_b)
        early = [heat_out(r, blocks[r // CHUNK], r % CHUNK) for r in range(2 * CHUNK)]
        for copy in early:
            copy.start()
        ahead = iter(range(-1, ROWS + 1))

        def between_one():
            for r in (next(ahead, None), next(ahead, None), next(ahead, None)):
                if r is not None:
                    step_one(r)

        rows = list(range(2 * CHUNK, 3 * CHUNK))
        network_chunk(rows, *net, put, between_one)
        late = [heat_out(r) for r in rows]
        for copy in late:
            copy.start()
        behind = iter(range(3 * CHUNK))

        def between_two():
            for r in (next(behind, None), next(behind, None)):
                if r is not None:
                    step_two(r, blocks[r // CHUNK][r % CHUNK] if r < 2 * CHUNK else heat_s[r])

        rows = list(range(3 * CHUNK, ROWS))
        network_chunk(rows, *net, put, between_two)
        for r in rows:
            copy = heat_out(r)
            copy.start()
            late.append(copy)
            step_two(r, heat_s[r])
        for copy in early + late:
            copy.wait()
        for r in range(ROWS):
            temp_out(r).wait()

    @pl.when(jnp.logical_not(every))
    def _():
        n = count_lit(lit_row, lit_s, info, list_sem)
        heat_s[...] = jnp.zeros_like(heat_s)
        for part, block in ((0, heat_a), (1, heat_b)):
            @pl.when(n > part * CHUNK)
            def _():
                for j in range(CHUNK):
                    heat_s[info[part * CHUNK + j]] = block[j]

        def one(c, _):
            network_chunk(listed(info, c), *net, put)
            return 0

        lax.fori_loop(2, (n + CHUNK - 1) // CHUNK, one, 0)
        for r in range(ROWS):
            heat_out(r).start()
        for r in range(-1, ROWS + 1):
            step_one(r)
            if r >= 1:
                step_two(r - 1, heat_s[r - 1])
        for r in range(ROWS):
            heat_out(r).wait()
        for r in range(ROWS):
            temp_out(r).wait()


def last(*arrays):
    whole = jax.ShapeDtypeStruct((LEV, ROWS, COLS), F32)
    track = pltpu.VMEM((ROWS, PAD, COLS), F32)
    return pl.pallas_call(
        last_kernel,
        out_shape=(whole, whole),
        in_specs=[VMEM] * 18,
        out_specs=(HBM, HBM),
        scratch_shapes=LIST_SCRATCH
        + [
            track,
            pltpu.VMEM((ROWS + 2, PAD, COLS), F32),
            track,
            pltpu.SemaphoreType.DMA((2,)),
        ],
        compiler_params=pltpu.CompilerParams(vmem_limit_bytes=32 << 20),
        cost_estimate=pl.CostEstimate(flops=10**10, bytes_accessed=8 * 10**6, transcendentals=0),
    )(*arrays)


def on_device(t, m, s, lit, k, w1, b1, w2, b2, w4, b4):
    lats, lons = lax.axis_size("lat"), lax.axis_size("lon")
    lit_row = jnp.concatenate([lit.reshape(1, ROWS), jnp.ones((1, COLS - ROWS), jnp.int32)], axis=1)
    t, m, *net, up, down, west, east = load(
        t, m, s, k, w1.T, b1.reshape(1, HID), w2, b2, w4, b4.reshape(1, LEV)
    )
    north = lax.ppermute(down, "lat", [(i, i + 1) for i in range(lats - 1)])
    south = lax.ppermute(up, "lat", [(i + 1, i) for i in range(lats - 1)])
    heat_a = some_rows(0, lit_row, t, m, *net)
    west, east = corners(north, south, west, east)
    from_east = lax.ppermute(west, "lon", [(i, (i - 1) % lons) for i in range(lons)])
    from_west = lax.ppermute(east, "lon", [(i, (i + 1) % lons) for i in range(lons)])
    heat_b = some_rows(1, lit_row, t, m, *net)
    return last(lit_row, t, m, *net, heat_a, heat_b, north, south, west, east, from_west, from_east)


def solution(mesh):
    whole, plane = P(None, "lat", "lon"), P("lat", "lon")
    return jax.shard_map(
        on_device,
        mesh=mesh,
        in_specs=(whole, whole, plane, plane, plane) + (P(),) * 6,
        out_specs=(whole, whole),
        check_vma=False,
    )
```

```python
import functools

import jax
import jax.numpy as jnp
from jax import lax
from jax.experimental import pallas as pl
from jax.experimental.pallas import tpu as pltpu
from jax.sharding import PartitionSpec as P

F32 = jnp.float32
BF16 = jnp.bfloat16
F8 = jnp.float8_e4m3fn

LEV = 90
PAD = 96
ROWS = 32
COLS = 128
HID = 512
FEAT = 181
KIN = 2 * PAD
CHUNK = 8
GROUPS = 4
W_LO = 2.0**15
W_HI = 2.0**6
X_LO = 2.0**9
NET_LIMIT = 32 << 20

VMEM = pl.BlockSpec(memory_space=pltpu.VMEM)
HBM = pl.BlockSpec(memory_space=pltpu.HBM)


def split(x):
    hi = x.astype(BF16)
    return hi, (x - hi.astype(F32)).astype(BF16)


def lane_index():
    return lax.broadcasted_iota(jnp.int32, (PAD, COLS), 1)


def put_split(hi_ref, eight_ref, w, n):
    hi = w.astype(BF16)
    hi_ref[...] = hi
    eight_ref[:, 0:n] = ((w - hi.astype(F32)) * W_LO).astype(F8)
    eight_ref[:, n : 2 * n] = (w * W_HI).astype(F8)


def column_of(row, n):
    hi = row.astype(BF16)
    rest = row - hi.astype(F32)
    mid = rest.astype(BF16)
    low = (rest - mid.astype(F32)).astype(BF16)
    parts = jnp.concatenate([hi, mid, low, jnp.zeros((13, n), BF16)], axis=0)
    return lax.dot_general(
        parts, jnp.ones((16, COLS), BF16), (((0,), (0,)), ((), ())), preferred_element_type=F32
    )


def power_below(bound):
    scale = jnp.float32(1.0)
    for k in range(9):
        scale = jnp.where(bound > 440.0 * 2.0**k, 0.5 ** (k + 1), scale)
    return scale


def prepare_outer(w1t, b1, b2, w4, b4, w1s, w18, w4s, bs, sc):
    gap = jnp.zeros((PAD - LEV, HID), F32)
    w1 = jnp.concatenate(
        [w1t[0:LEV], gap, w1t[LEV:FEAT], b1[...], gap[0 : PAD - LEV - 2]], axis=0
    )
    put_split(w1s, w18, jnp.transpose(w1 * 0.5), KIN)
    hi, lo = split(jnp.concatenate([w4[...], gap], axis=0))
    w4s[0:PAD] = hi
    w4s[PAD:] = lo
    for k in range(2):
        bs[k * HID : (k + 1) * HID] = column_of(b2[k : k + 1] * 0.5, HID)
    bs[2 * HID : 2 * HID + PAD] = jnp.concatenate(
        [column_of(b4[...], LEV), jnp.zeros((PAD - LEV, COLS), F32)], axis=0
    )
    bound = 6.0 * jnp.max(jnp.sum(jnp.abs(w1), axis=0, keepdims=True))
    put_scale(sc, 0, bound)
    return bound


def put_scale(sc, k, bound):
    scale = power_below(bound)
    sc[k : k + 1] = jnp.full((1, COLS), scale)
    sc[k + 2 : k + 3] = jnp.full((1, COLS), 1.0 / (W_LO * scale))


def prepare_inner(k, w2, w2s, w28):
    put_split(w2s.at[k], w28.at[k], w2[k] * 0.5, HID)


def first_columns(block, r, west, east):
    lane = lane_index()
    place = 2 * (r + 1)
    here = (lane == place) | (lane == place + 1)
    rolled = pltpu.roll(block, place, 1) if place else block
    return jnp.where(here, rolled, west), jnp.where(here, pltpu.roll(block, place + 2, 1), east)


def rows_in(src, dst, sem):
    return [pltpu.make_async_copy(src.at[:, r, :], dst.at[r, pl.ds(0, LEV), :], sem) for r in range(ROWS)]


def pack_kernel(t_hbm, k_hbm, t, pay_a, pay_b, west_out, east_out, k, sem):
    copies = [pltpu.make_async_copy(k_hbm, k, sem)] + rows_in(t_hbm, t, sem)
    for copy in copies:
        copy.start()
    pay_b[PAD:] = jnp.zeros((PAY_B - PAD, COLS), F32)
    for copy in copies:
        copy.wait()
    blank = jnp.zeros((PAD - LEV - 1, COLS), F32)
    west = jnp.zeros((PAD, COLS), F32)
    east = jnp.zeros((PAD, COLS), F32)
    for r in range(ROWS):
        t[r, LEV:PAD, :] = jnp.concatenate([k[r : r + 1, :], blank], axis=0)
        west, east = first_columns(t[r], r, west, east)
    west_out[...] = west
    east_out[...] = east
    for i, r in enumerate((ROWS - 1, ROWS - 2, 0, 1)):
        pay_a[i * PAD : (i + 1) * PAD] = t[r]
    even = lax.axis_index("lon") % 2 == 0
    pay_a[4 * PAD : 5 * PAD] = jnp.where(even, east, west)
    pay_b[0:PAD] = jnp.where(even, west, east)


def in_hbm(*arrays):
    return [pltpu.with_memory_space_constraint(x, pltpu.HBM) for x in arrays]


TRACK = jax.ShapeDtypeStruct((ROWS, PAD, COLS), F32)
PAY_A = 5 * PAD
PAY_B = 256
SIDE = jax.ShapeDtypeStruct((PAD, COLS), F32)
def pack(t, k):
    return pl.pallas_call(
        pack_kernel,
        out_shape=(
            TRACK,
            jax.ShapeDtypeStruct((PAY_A, COLS), F32),
            jax.ShapeDtypeStruct((PAY_B, COLS), F32),
            SIDE,
            SIDE,
        ),
        in_specs=[HBM] * 2,
        out_specs=(VMEM,) * 5,
        scratch_shapes=[pltpu.VMEM((ROWS, COLS), F32), pltpu.SemaphoreType.DMA],
        compiler_params=pltpu.CompilerParams(vmem_limit_bytes=16 << 20),
        cost_estimate=pl.CostEstimate(flops=10**6, bytes_accessed=4 * 10**6, transcendentals=0),
    )(*in_hbm(t, k))


def all_lit(lit_row):
    return jnp.min(lit_row[...].astype(F32)) > 0.5


def lit_rows(lit_ref, info):
    for r in range(ROWS):
        info[r] = 0

    def step(r, carry):
        n, last = carry
        lit = lit_ref[0, r] > 0

        @pl.when(lit)
        def _():
            info[n] = r

        return jnp.where(lit, n + 1, n), jnp.where(lit, r, last)

    n, last = lax.fori_loop(0, ROWS, step, (jnp.int32(0), jnp.int32(0)))

    def fill(i, _):
        info[i] = last
        return 0

    lax.fori_loop(n, ROWS, fill, 0)
    info[ROWS] = n


def count_lit(lit_row, lit_s, info, sem):
    copy = pltpu.make_async_copy(lit_row, lit_s, sem)
    copy.start()
    copy.wait()
    lit_rows(lit_s, info)
    return info[ROWS]


LIST_SCRATCH = [
    pltpu.SMEM((1, COLS), jnp.int32),
    pltpu.SMEM((ROWS + 8,), jnp.int32),
    pltpu.SemaphoreType.DMA,
]


def half_silu(u):
    return u + u * jnp.tanh(u)


def out_layer(w4s, x):
    hi, lo = split(x)
    both = jnp.dot(w4s[...], hi, preferred_element_type=F32)
    return both[0:PAD] + both[PAD:] + jnp.dot(w4s[0:PAD], lo, preferred_element_type=F32)


def parts8(x, scale):
    hi = x.astype(BF16)
    low = x - hi.astype(F32)
    scaled = x if scale is None else x * scale
    factor = X_LO if scale is None else scale * X_LO
    return hi, jnp.concatenate([scaled.astype(F8), (low * factor).astype(F8)], axis=0)


def dot8(w, w8, held, back):
    hi, eight = held
    v = jnp.dot(w, hi, preferred_element_type=F32)
    return v + jnp.dot(w8, eight, preferred_element_type=F32) * back


def network_chunk(rows, t, m, w1s, w18, w2s, w28, w4s, bs, sc, put, between=lambda: None):
    n = CHUNK // GROUPS
    tile = lambda b: jnp.concatenate([b] * n, axis=1)
    scale = [tile(sc[k : k + 1]) for k in range(2)]
    back = [tile(sc[k : k + 1]) for k in range(2, 4)]
    held = [None] * GROUPS
    for g in range(GROUPS):
        x = jnp.concatenate(
            [jnp.concatenate([t[r], m[r]], axis=0) for r in rows[g * n : (g + 1) * n]], axis=1
        )
        v = dot8(w1s[...], w18[...], parts8(x, None), 1.0 / W_LO)
        held[g] = parts8(half_silu(v), scale[0])
        between()
    for k in range(2):
        for g in range(GROUPS):
            v = dot8(w2s[k], w28[k], held[g], back[k])
            h = half_silu(v + tile(bs[k * HID : (k + 1) * HID]))
            held[g] = parts8(h, scale[1]) if k == 0 else h
            between()
    for g in range(GROUPS):
        o = out_layer(w4s, held[g]) + tile(bs[2 * HID : 2 * HID + PAD])
        for j in range(n):
            row = rows[g * n + j]
            put(g * n + j, row, o[:, j * COLS : (j + 1) * COLS] * m[row, LEV : LEV + 1, :])
        between()


def listed(info, c):
    return [info[c * CHUNK + j] for j in range(CHUNK)]


def heat_kernel(
    lit_row, t, m_hbm, s_hbm, w1_hbm, b1_hbm, w2_hbm, b2_hbm, w4_hbm, b4_hbm, heat,
    m, w1s, w18, w2s, w28, w4s, bs, sc, s, w1, b1, w2, b2, w4, b4, lit_s, info, sem, sems,
):
    every = all_lit(lit_row)
    pairs = ((w1_hbm, w1), (b1_hbm, b1), (b2_hbm, b2), (w4_hbm, w4), (b4_hbm, b4))
    outer = [pltpu.make_async_copy(a, b, sems.at[0]) for a, b in pairs]
    inner = [pltpu.make_async_copy(w2_hbm.at[i], w2.at[i], sems.at[1 + i]) for i in range(2)]
    humid = [pltpu.make_async_copy(s_hbm, s, sems.at[3])] + rows_in(m_hbm, m, sems.at[3])
    for copy in outer + inner + humid:
        copy.start()

    @pl.when(every)
    def _():
        for r in range(ROWS):
            info[r] = r
        info[ROWS] = ROWS

    @pl.when(jnp.logical_not(every))
    def _():
        count_lit(lit_row, lit_s, info, sem)
        heat[...] = jnp.zeros_like(heat)

    for copy in outer:
        copy.wait()
    bound = prepare_outer(w1, b1, b2, w4, b4, w1s, w18, w4s, bs, sc)
    inner[0].wait()
    prepare_inner(0, w2, w2s, w28)
    bound = bound * jnp.max(jnp.sum(jnp.abs(w2[0]), axis=1, keepdims=True)) + jnp.max(jnp.abs(b2[...]))
    put_scale(sc, 1, bound)
    inner[1].wait()
    prepare_inner(1, w2, w2s, w28)
    for copy in humid:
        copy.wait()
    last_levels = jnp.concatenate([jnp.ones((1, COLS), F32), jnp.zeros((PAD - LEV - 2, COLS), F32)], axis=0)
    for r in range(ROWS):
        m[r, LEV:PAD, :] = jnp.concatenate([s[r : r + 1, :], last_levels], axis=0)

    def put(j, row, value):
        heat[row] = value

    def one(c, _):
        network_chunk(listed(info, c), t, m, w1s, w18, w2s, w28, w4s, bs, sc, put)
        return 0

    lax.fori_loop(0, (info[ROWS] + CHUNK - 1) // CHUNK, one, 0)


WEIGHTS = (
    ((HID, KIN), BF16),
    ((HID, 2 * KIN), F8),
    ((2, HID, HID), BF16),
    ((2, HID, 2 * HID), F8),
    ((2 * PAD, HID), BF16),
    ((2 * HID + PAD, COLS), F32),
    ((8, COLS), F32),
)


def heat_of(lit_row, t, *arrays):
    return pl.pallas_call(
        heat_kernel,
        out_shape=TRACK,
        in_specs=[VMEM] * 2 + [HBM] * 8,
        out_specs=VMEM,
        scratch_shapes=[pltpu.VMEM((ROWS, PAD, COLS), F32)]
        + [pltpu.VMEM(*shape) for shape in WEIGHTS]
        + [
            pltpu.VMEM((ROWS, COLS), F32),
            pltpu.VMEM((FEAT, HID), F32),
            pltpu.VMEM((1, HID), F32),
            pltpu.VMEM((2, HID, HID), F32),
            pltpu.VMEM((2, HID), F32),
            pltpu.VMEM((LEV, HID), F32),
            pltpu.VMEM((1, LEV), F32),
        ]
        + LIST_SCRATCH
        + [pltpu.SemaphoreType.DMA((4,))],
        compiler_params=pltpu.CompilerParams(vmem_limit_bytes=NET_LIMIT),
        cost_estimate=pl.CostEstimate(flops=2 * 10**10, bytes_accessed=8 * 10**6, transcendentals=0),
    )(lit_row, t, *in_hbm(*arrays))


def diffuse_kernel(
    t, heat, gather_a, gather_b, mine_w, mine_e, heat_hbm, temp_hbm, edges, sides, step_s, temp_s, sems,
):
    lat, lats = lax.axis_index("lat"), lax.axis_size("lat")
    even = lax.axis_index("lon") % 2 == 0
    above, below = jnp.maximum(lat - 1, 0), jnp.minimum(lat + 1, lats - 1)
    mine = jnp.where(even, 0, lats)
    other = lats - mine

    def fetch(src, place, start, count, dst):
        return pltpu.make_async_copy(src.at[place, pl.ds(start, count)], dst, sems.at[0])

    copies = [
        fetch(gather_a, mine + above, 0, 2 * PAD, edges.at[0]),
        fetch(gather_a, mine + below, 2 * PAD, 2 * PAD, edges.at[1]),
    ]
    for i, row in enumerate((above, lat, below)):
        copies.append(fetch(gather_a, other + row, 4 * PAD, PAD, sides.at[i]))
        copies.append(fetch(gather_b, mine + row, 0, PAD, sides.at[3 + i]))
    for copy in copies:
        copy.start()

    def heat_out(r):
        return pltpu.make_async_copy(heat.at[r, pl.ds(0, LEV), :], heat_hbm.at[:, r, :], sems.at[1])

    def temp_out(r):
        return pltpu.make_async_copy(temp_s.at[r, pl.ds(0, LEV), :], temp_hbm.at[:, r, :], sems.at[2])

    for r in range(ROWS):
        heat_out(r).start()
    for copy in copies:
        copy.wait()
    lane = lane_index()
    top = jnp.where(lat > 0, 1.0, 0.0).astype(F32)
    bottom = jnp.where(lat < lats - 1, 1.0, 0.0).astype(F32)
    edges[0] = edges[0] * top
    edges[1] = edges[1] * bottom

    def column(i):
        before = pltpu.roll(sides[i], COLS // 2, 1) * top
        after = pltpu.roll(sides[i + 2], COLS // 2, 1) * bottom
        return jnp.where(lane < 2, before, jnp.where(lane < 2 * (ROWS + 1), sides[i + 1], after))

    in_a, in_b = column(0), column(3)
    west, east = jnp.where(even, in_b, in_a), jnp.where(even, in_a, in_b)

    def state(r):
        if r < 0:
            return edges[0, 0:PAD] if r == -1 else edges[0, PAD : 2 * PAD]
        if r >= ROWS:
            return edges[1, 0:PAD] if r == ROWS else edges[1, PAD : 2 * PAD]
        return t[r]

    def number(r):
        if r < 0:
            return edges[0, LEV : LEV + 1]
        if r >= ROWS:
            return edges[1, LEV : LEV + 1]
        return t[r, LEV : LEV + 1, :]

    odd = lane % 2 == 1
    side = jnp.where(odd, west, east)

    def compact(far, own, towards):
        near = far
        number = near[LEV : LEV + 1, :]
        around = (
            pltpu.roll(near, 2, 1)
            + pltpu.roll(near, COLS - 2, 1)
            + pltpu.roll(near, towards, 1)
            + pltpu.roll(own[...], towards, 1)
        )
        return near + number * (around - 4.0 * near)

    side_next = jnp.where(odd, compact(west, mine_w, 1), compact(east, mine_e, COLS - 1))
    first_lane, last_lane = lane == 0, lane == COLS - 1

    def substep(above, here, below, number, sides, r):
        edge = pltpu.roll(sides, (-(2 * r + 3)) % COLS, 1)
        left = jnp.where(first_lane, edge, pltpu.roll(here, 1, 1))
        right = jnp.where(last_lane, edge, pltpu.roll(here, COLS - 1, 1))
        return here + number * (above + below + left + right - 4.0 * here)

    for r in range(-1, ROWS + 1):
        step_s[r + 1] = substep(state(r - 1), state(r), state(r + 1), number(r), side, r)
        if r >= 1:
            q = r - 1
            done = substep(step_s[q], step_s[q + 1], step_s[q + 2], number(q), side_next, q)
            temp_s[q] = done + heat[q]
            temp_out(q).start()
    for r in range(ROWS):
        heat_out(r).wait()
    for r in range(ROWS):
        temp_out(r).wait()


def diffuse(t, heat, gather_a, gather_b, mine_w, mine_e):
    whole = jax.ShapeDtypeStruct((LEV, ROWS, COLS), F32)
    return pl.pallas_call(
        diffuse_kernel,
        out_shape=(whole, whole),
        in_specs=[VMEM, VMEM, HBM, HBM, VMEM, VMEM],
        out_specs=(HBM, HBM),
        scratch_shapes=[
            pltpu.VMEM((2, 2 * PAD, COLS), F32),
            pltpu.VMEM((6, PAD, COLS), F32),
            pltpu.VMEM((ROWS + 2, PAD, COLS), F32),
            pltpu.VMEM((ROWS, PAD, COLS), F32),
            pltpu.SemaphoreType.DMA((3,)),
        ],
        compiler_params=pltpu.CompilerParams(vmem_limit_bytes=16 << 20),
        cost_estimate=pl.CostEstimate(flops=10**7, bytes_accessed=8 * 10**6, transcendentals=0),
    )(t, heat, *in_hbm(gather_a, gather_b), mine_w, mine_e)


def on_device(t, m, s, lit, k, w1, b1, w2, b2, w4, b4):
    lats, lons = lax.axis_size("lat"), lax.axis_size("lon")
    lit_row = jnp.concatenate([lit.reshape(1, ROWS), jnp.ones((1, COLS - ROWS), jnp.int32)], axis=1)
    t, pay_a, pay_b, west, east = pack(t, k)

    def group(first):
        pair = [first, (first + 1) % lons]
        return [lon * lats + lat for lon in pair for lat in range(lats)]

    gather_a = lax.all_gather(pay_a, ("lon", "lat"), axis_index_groups=[group(i) for i in range(0, lons, 2)])
    gather_b = lax.all_gather(pay_b, ("lon", "lat"), axis_index_groups=[group(i) for i in range(1, lons, 2)])
    heat = heat_of(lit_row, t, m, s, w1.T, b1.reshape(1, HID), w2, b2, w4, b4.reshape(1, LEV))
    return diffuse(t, heat, gather_a, gather_b, west, east)


def solution(mesh):
    whole, plane = P(None, "lat", "lon"), P("lat", "lon")
    return jax.shard_map(
        on_device,
        mesh=mesh,
        in_specs=(whole, whole, plane, plane, plane) + (P(),) * 6,
        out_specs=(whole, whole),
        check_vma=False,
    )
```

```python
import functools

import jax
import jax.numpy as jnp
from jax import lax
from jax.experimental import pallas as pl
from jax.experimental.pallas import tpu as pltpu
from jax.sharding import PartitionSpec as P

F32 = jnp.float32
BF16 = jnp.bfloat16
F8 = jnp.float8_e4m3fn

LEV = 90
PAD = 96
ROWS = 32
COLS = 128
HID = 512
FEAT = 181
KIN = 2 * PAD
CHUNK = 8
GROUPS = 4
EARLY = 2
W_LO = 2.0**15
W_HI = 2.0**6
X_LO = 2.0**9
LOAD_LIMIT = 32 << 20

VMEM = pl.BlockSpec(memory_space=pltpu.VMEM)
HBM = pl.BlockSpec(memory_space=pltpu.HBM)


def split(x):
    hi = x.astype(BF16)
    return hi, (x - hi.astype(F32)).astype(BF16)


def lane_index():
    return lax.broadcasted_iota(jnp.int32, (PAD, COLS), 1)


def put_split(hi_ref, eight_ref, w, n):
    hi = w.astype(BF16)
    hi_ref[...] = hi
    eight_ref[:, 0:n] = ((w - hi.astype(F32)) * W_LO).astype(F8)
    eight_ref[:, n : 2 * n] = (w * W_HI).astype(F8)


def column_of(row, n):
    hi = row.astype(BF16)
    rest = row - hi.astype(F32)
    mid = rest.astype(BF16)
    low = (rest - mid.astype(F32)).astype(BF16)
    parts = jnp.concatenate([hi, mid, low, jnp.zeros((13, n), BF16)], axis=0)
    return lax.dot_general(
        parts, jnp.ones((16, COLS), BF16), (((0,), (0,)), ((), ())), preferred_element_type=F32
    )


def power_below(bound):
    scale = jnp.float32(1.0)
    for k in range(9):
        scale = jnp.where(bound > 440.0 * 2.0**k, 0.5 ** (k + 1), scale)
    return scale


def prepare_outer(w1t, b1, b2, w4, b4, w1s, w18, w4s, bs, sc):
    gap = jnp.zeros((PAD - LEV, HID), F32)
    w1 = jnp.concatenate(
        [w1t[0:LEV], gap, w1t[LEV:FEAT], b1[...], gap[0 : PAD - LEV - 2]], axis=0
    )
    put_split(w1s, w18, jnp.transpose(w1 * 0.5), KIN)
    hi, lo = split(jnp.concatenate([w4[...], gap], axis=0))
    w4s[0:PAD] = hi
    w4s[PAD:] = lo
    for k in range(2):
        bs[k * HID : (k + 1) * HID] = column_of(b2[k : k + 1] * 0.5, HID)
    bs[2 * HID : 2 * HID + PAD] = jnp.concatenate(
        [column_of(b4[...], LEV), jnp.zeros((PAD - LEV, COLS), F32)], axis=0
    )
    bound = 6.0 * jnp.max(jnp.sum(jnp.abs(w1), axis=0, keepdims=True))
    put_scale(sc, 0, bound)
    return bound


def put_scale(sc, k, bound):
    scale = power_below(bound)
    sc[k : k + 1] = jnp.full((1, COLS), scale)
    sc[k + 2 : k + 3] = jnp.full((1, COLS), 1.0 / (W_LO * scale))


def prepare_inner(k, w2, w2s, w28):
    put_split(w2s.at[k], w28.at[k], w2[k] * 0.5, HID)


def first_columns(block, r, west, east):
    lane = lane_index()
    place = 2 * (r + 1)
    here = (lane == place) | (lane == place + 1)
    rolled = pltpu.roll(block, place, 1) if place else block
    return jnp.where(here, rolled, west), jnp.where(here, pltpu.roll(block, place + 2, 1), east)


def load_kernel(
    t_hbm, m_hbm, s_hbm, k_hbm, w1_hbm, b1_hbm, w2_hbm, b2_hbm, w4_hbm, b4_hbm,
    t, m, w1s, w18, w2s, w28, w4s, bs, sc, up, down, west_out, east_out,
    k, s, w1, b1, w2, b2, w4, b4, sems,
):
    def rows(src, dst, sem):
        return [pltpu.make_async_copy(src.at[:, r, :], dst.at[r, pl.ds(0, LEV), :], sem) for r in range(ROWS)]

    pairs = ((w1_hbm, w1), (b1_hbm, b1), (b2_hbm, b2), (w4_hbm, w4), (b4_hbm, b4))
    outer = [pltpu.make_async_copy(a, b, sems.at[0]) for a, b in pairs]
    state = [pltpu.make_async_copy(k_hbm, k, sems.at[1])] + rows(t_hbm, t, sems.at[1])
    inner = [pltpu.make_async_copy(w2_hbm.at[i], w2.at[i], sems.at[2 + i]) for i in range(2)]
    humid = [pltpu.make_async_copy(s_hbm, s, sems.at[4])] + rows(m_hbm, m, sems.at[4])
    for copy in outer + state + inner + humid:
        copy.start()
    for copy in outer:
        copy.wait()
    bound = prepare_outer(w1, b1, b2, w4, b4, w1s, w18, w4s, bs, sc)
    for copy in state:
        copy.wait()
    blank = jnp.zeros((PAD - LEV - 1, COLS), F32)
    west = jnp.zeros((PAD, COLS), F32)
    east = jnp.zeros((PAD, COLS), F32)
    for r in range(ROWS):
        t[r, LEV:PAD, :] = jnp.concatenate([k[r : r + 1, :], blank], axis=0)
        west, east = first_columns(t[r], r, west, east)
    west_out[...] = west
    east_out[...] = east
    up[0:PAD] = t[0]
    up[PAD:] = t[1]
    down[0:PAD] = t[ROWS - 1]
    down[PAD:] = t[ROWS - 2]
    inner[0].wait()
    prepare_inner(0, w2, w2s, w28)
    bound = bound * jnp.max(jnp.sum(jnp.abs(w2[0]), axis=1, keepdims=True)) + jnp.max(jnp.abs(b2[...]))
    put_scale(sc, 1, bound)
    inner[1].wait()
    prepare_inner(1, w2, w2s, w28)
    for copy in humid:
        copy.wait()
    one = jnp.ones((1, COLS), F32)
    for r in range(ROWS):
        m[r, LEV:PAD, :] = jnp.concatenate([s[r : r + 1, :], one, blank[1:]], axis=0)


TRACK = jax.ShapeDtypeStruct((ROWS, PAD, COLS), F32)
EDGE = jax.ShapeDtypeStruct((2 * PAD, COLS), F32)
SIDE = jax.ShapeDtypeStruct((PAD, COLS), F32)
WEIGHTS = (
    ((HID, KIN), BF16),
    ((HID, 2 * KIN), F8),
    ((2, HID, HID), BF16),
    ((2, HID, 2 * HID), F8),
    ((2 * PAD, HID), BF16),
    ((2 * HID + PAD, COLS), F32),
    ((8, COLS), F32),
)


def load(*arrays):
    return pl.pallas_call(
        load_kernel,
        out_shape=(TRACK, TRACK)
        + tuple(jax.ShapeDtypeStruct(*w) for w in WEIGHTS)
        + (EDGE, EDGE, SIDE, SIDE),
        in_specs=[HBM] * 10,
        out_specs=(VMEM,) * 13,
        scratch_shapes=[
            pltpu.VMEM((ROWS, COLS), F32),
            pltpu.VMEM((ROWS, COLS), F32),
            pltpu.VMEM((FEAT, HID), F32),
            pltpu.VMEM((1, HID), F32),
            pltpu.VMEM((2, HID, HID), F32),
            pltpu.VMEM((2, HID), F32),
            pltpu.VMEM((LEV, HID), F32),
            pltpu.VMEM((1, LEV), F32),
            pltpu.SemaphoreType.DMA((5,)),
        ],
        compiler_params=pltpu.CompilerParams(vmem_limit_bytes=LOAD_LIMIT),
        cost_estimate=pl.CostEstimate(flops=10**6, bytes_accessed=8 * 10**6, transcendentals=0),
    )(*(pltpu.with_memory_space_constraint(x, pltpu.HBM) for x in arrays))


def corner_kernel(north_ref, south_ref, west_ref, east_ref, w_out, e_out):
    west, east = west_ref[...], east_ref[...]
    west, east = first_columns(north_ref[0:PAD], -1, west, east)
    west, east = first_columns(south_ref[0:PAD], ROWS, west, east)
    w_out[...] = west
    e_out[...] = east


def corners(north, south, west, east):
    side = jax.ShapeDtypeStruct((PAD, COLS), F32)
    return pl.pallas_call(
        corner_kernel,
        out_shape=(side, side),
        in_specs=[VMEM] * 4,
        out_specs=(VMEM, VMEM),
        compiler_params=pltpu.CompilerParams(vmem_limit_bytes=8 << 20),
        cost_estimate=pl.CostEstimate(flops=10**5, bytes_accessed=4 * 10**5, transcendentals=0),
    )(north, south, west, east)


def all_lit(lit_row):
    return jnp.min(lit_row[...].astype(F32)) > 0.5


def lit_rows(lit_ref, info):
    for r in range(ROWS):
        info[r] = 0

    def step(r, carry):
        n, last = carry
        lit = lit_ref[0, r] > 0

        @pl.when(lit)
        def _():
            info[n] = r

        return jnp.where(lit, n + 1, n), jnp.where(lit, r, last)

    n, last = lax.fori_loop(0, ROWS, step, (jnp.int32(0), jnp.int32(0)))

    def fill(i, _):
        info[i] = last
        return 0

    lax.fori_loop(n, ROWS, fill, 0)
    info[ROWS] = n


def count_lit(lit_row, lit_s, info, sem):
    copy = pltpu.make_async_copy(lit_row, lit_s, sem)
    copy.start()
    copy.wait()
    lit_rows(lit_s, info)
    return info[ROWS]


LIST_SCRATCH = [
    pltpu.SMEM((1, COLS), jnp.int32),
    pltpu.SMEM((ROWS + 8,), jnp.int32),
    pltpu.SemaphoreType.DMA,
]


def half_silu(u):
    return u + u * jnp.tanh(u)


def out_layer(w4s, x):
    hi, lo = split(x)
    both = jnp.dot(w4s[...], hi, preferred_element_type=F32)
    return both[0:PAD] + both[PAD:] + jnp.dot(w4s[0:PAD], lo, preferred_element_type=F32)


def parts8(x, scale):
    hi = x.astype(BF16)
    low = x - hi.astype(F32)
    scaled = x if scale is None else x * scale
    factor = X_LO if scale is None else scale * X_LO
    return hi, jnp.concatenate([scaled.astype(F8), (low * factor).astype(F8)], axis=0)


def dot8(w, w8, held, back):
    hi, eight = held
    v = jnp.dot(w, hi, preferred_element_type=F32)
    return v + jnp.dot(w8, eight, preferred_element_type=F32) * back


def network_chunk(rows, t, m, w1s, w18, w2s, w28, w4s, bs, sc, put, between=lambda: None):
    n = CHUNK // GROUPS
    tile = lambda b: jnp.concatenate([b] * n, axis=1)
    scale = [tile(sc[k : k + 1]) for k in range(2)]
    back = [tile(sc[k : k + 1]) for k in range(2, 4)]
    held = [None] * GROUPS
    for g in range(GROUPS):
        x = jnp.concatenate(
            [jnp.concatenate([t[r], m[r]], axis=0) for r in rows[g * n : (g + 1) * n]], axis=1
        )
        v = dot8(w1s[...], w18[...], parts8(x, None), 1.0 / W_LO)
        held[g] = parts8(half_silu(v), scale[0])
        between()
    for k in range(2):
        for g in range(GROUPS):
            v = dot8(w2s[k], w28[k], held[g], back[k])
            h = half_silu(v + tile(bs[k * HID : (k + 1) * HID]))
            held[g] = parts8(h, scale[1]) if k == 0 else h
            between()
    for g in range(GROUPS):
        o = out_layer(w4s, held[g]) + tile(bs[2 * HID : 2 * HID + PAD])
        for j in range(n):
            row = rows[g * n + j]
            put(g * n + j, row, o[:, j * COLS : (j + 1) * COLS] * m[row, LEV : LEV + 1, :])
        between()


def listed(info, c):
    return [info[c * CHUNK + j] for j in range(CHUNK)]


def starts_early():
    return lax.axis_index("lon") < EARLY


def list_or_all(lit_row, lit_s, info, sem):
    every = all_lit(lit_row)

    @pl.when(every)
    def _():
        for r in range(ROWS):
            info[r] = r
        info[ROWS] = ROWS

    @pl.when(jnp.logical_not(every))
    def _():
        count_lit(lit_row, lit_s, info, sem)

    return info[ROWS]


def before_kernel(lit_row, t, m, w1s, w18, w2s, w28, w4s, bs, sc, out, lit_s, info, sem):
    n = list_or_all(lit_row, lit_s, info, sem)
    chunks = jnp.minimum((n + CHUNK - 1) // CHUNK, jnp.where(starts_early(), 2, 1))

    def one(c, _):
        def put(j, row, value):
            out[c * CHUNK + j] = value

        network_chunk(listed(info, c), t, m, w1s, w18, w2s, w28, w4s, bs, sc, put)
        return 0

    lax.fori_loop(0, chunks, one, 0)


def after_kernel(lit_row, before, t, m, w1s, w18, w2s, w28, w4s, bs, sc, out, lit_s, info, sem):
    n = list_or_all(lit_row, lit_s, info, sem)
    early = starts_early()

    @pl.when(early)
    def _():
        out[0:CHUNK] = before[CHUNK : 2 * CHUNK]

    def one(c, _):
        def put(j, row, value):
            out[(c - 1) * CHUNK + j] = value

        network_chunk(listed(info, c), t, m, w1s, w18, w2s, w28, w4s, bs, sc, put)
        return 0

    start = jnp.where(early, 2, 1)
    lax.fori_loop(start, jnp.minimum((n + CHUNK - 1) // CHUNK, 2 * start), one, 0)


def some_rows(kernel, blocks, *arrays):
    return pl.pallas_call(
        kernel,
        out_shape=jax.ShapeDtypeStruct((blocks * CHUNK, PAD, COLS), F32),
        in_specs=[VMEM] * len(arrays),
        out_specs=VMEM,
        scratch_shapes=LIST_SCRATCH,
        compiler_params=pltpu.CompilerParams(vmem_limit_bytes=32 << 20),
        cost_estimate=pl.CostEstimate(flops=5 * 10**9, bytes_accessed=8 * 10**6, transcendentals=0),
    )(*arrays)


def last_kernel(
    lit_row, t, m, w1s, w18, w2s, w28, w4s, bs, sc, heat_a, heat_b, north, south, mine_w, mine_e, west, east,
    heat_hbm, temp_hbm, lit_s, info, list_sem, heat_s, step_s, temp_s, sems,
):
    net = (t, m, w1s, w18, w2s, w28, w4s, bs, sc)
    early = starts_early()
    fused = jnp.logical_and(all_lit(lit_row), jnp.logical_not(early))

    def heat_out(r, src=None, at=None):
        src, at = (heat_s, r) if src is None else (src, at)
        return pltpu.make_async_copy(src.at[at, pl.ds(0, LEV), :], heat_hbm.at[:, r, :], sems.at[0])

    def temp_out(r):
        return pltpu.make_async_copy(temp_s.at[r, pl.ds(0, LEV), :], temp_hbm.at[:, r, :], sems.at[1])

    def put(j, row, value):
        heat_s[row] = value

    def state(r):
        if r < 0:
            return north[0:PAD] if r == -1 else north[PAD:]
        if r >= ROWS:
            return south[0:PAD] if r == ROWS else south[PAD:]
        return t[r]

    def number(r):
        if r < 0:
            return north[LEV : LEV + 1]
        if r >= ROWS:
            return south[LEV : LEV + 1]
        return t[r, LEV : LEV + 1, :]

    lane = lane_index()
    odd = lane % 2 == 1
    side = jnp.where(odd, west[...], east[...])

    def compact(far, own, towards):
        near = far[...]
        number = near[LEV : LEV + 1, :]
        around = (
            pltpu.roll(near, 2, 1)
            + pltpu.roll(near, COLS - 2, 1)
            + pltpu.roll(near, towards, 1)
            + pltpu.roll(own[...], towards, 1)
        )
        return near + number * (around - 4.0 * near)

    side_next = jnp.where(odd, compact(west, mine_w, 1), compact(east, mine_e, COLS - 1))
    first_lane, last_lane = lane == 0, lane == COLS - 1

    def substep(above, here, below, number, sides, r):
        edge = pltpu.roll(sides, (-(2 * r + 3)) % COLS, 1)
        left = jnp.where(first_lane, edge, pltpu.roll(here, 1, 1))
        right = jnp.where(last_lane, edge, pltpu.roll(here, COLS - 1, 1))
        return here + number * (above + below + left + right - 4.0 * here)

    def step_one(r):
        step_s[r + 1] = substep(state(r - 1), state(r), state(r + 1), number(r), side, r)

    def step_two(r, heat):
        done = substep(step_s[r], step_s[r + 1], step_s[r + 2], number(r), side_next, r)
        temp_s[r] = done + heat
        temp_out(r).start()

    @pl.when(fused)
    def _():
        blocks = (heat_a, heat_b)
        early = [heat_out(r, blocks[r // CHUNK], r % CHUNK) for r in range(2 * CHUNK)]
        for copy in early:
            copy.start()
        ahead = iter(range(-1, ROWS + 1))

        def between_one():
            for r in (next(ahead, None), next(ahead, None), next(ahead, None)):
                if r is not None:
                    step_one(r)

        rows = list(range(2 * CHUNK, 3 * CHUNK))
        network_chunk(rows, *net, put, between_one)
        late = [heat_out(r) for r in rows]
        for copy in late:
            copy.start()
        behind = iter(range(3 * CHUNK))

        def between_two():
            for r in (next(behind, None), next(behind, None)):
                if r is not None:
                    step_two(r, blocks[r // CHUNK][r % CHUNK] if r < 2 * CHUNK else heat_s[r])

        rows = list(range(3 * CHUNK, ROWS))
        network_chunk(rows, *net, put, between_two)
        for r in rows:
            copy = heat_out(r)
            copy.start()
            late.append(copy)
            step_two(r, heat_s[r])
        for copy in early + late:
            copy.wait()
        for r in range(ROWS):
            temp_out(r).wait()

    @pl.when(jnp.logical_not(fused))
    def _():
        n = list_or_all(lit_row, lit_s, info, list_sem)
        chunks = (n + CHUNK - 1) // CHUNK

        @pl.when(n < ROWS)
        def _():
            heat_s[...] = jnp.zeros_like(heat_s)

        for part in range(ROWS // CHUNK):
            @pl.when(jnp.logical_and(part < chunks, jnp.logical_or(early, part < 2)))
            def _():
                for j in range(CHUNK):
                    block = heat_a[j] if part == 0 else heat_b[(part - 1) * CHUNK + j]
                    heat_s[info[part * CHUNK + j]] = block

        def one(c, _):
            network_chunk(listed(info, c), *net, put)
            return 0

        lax.fori_loop(jnp.where(early, chunks, 2), chunks, one, 0)
        for r in range(ROWS):
            heat_out(r).start()
        for r in range(-1, ROWS + 1):
            step_one(r)
            if r >= 1:
                step_two(r - 1, heat_s[r - 1])
        for r in range(ROWS):
            heat_out(r).wait()
        for r in range(ROWS):
            temp_out(r).wait()


def last(*arrays):
    whole = jax.ShapeDtypeStruct((LEV, ROWS, COLS), F32)
    track = pltpu.VMEM((ROWS, PAD, COLS), F32)
    return pl.pallas_call(
        last_kernel,
        out_shape=(whole, whole),
        in_specs=[VMEM] * 18,
        out_specs=(HBM, HBM),
        scratch_shapes=LIST_SCRATCH
        + [
            track,
            pltpu.VMEM((ROWS + 2, PAD, COLS), F32),
            track,
            pltpu.SemaphoreType.DMA((2,)),
        ],
        compiler_params=pltpu.CompilerParams(vmem_limit_bytes=32 << 20),
        cost_estimate=pl.CostEstimate(flops=10**10, bytes_accessed=8 * 10**6, transcendentals=0),
    )(*arrays)


def on_device(t, m, s, lit, k, w1, b1, w2, b2, w4, b4):
    lats, lons = lax.axis_size("lat"), lax.axis_size("lon")
    lit_row = jnp.concatenate([lit.reshape(1, ROWS), jnp.ones((1, COLS - ROWS), jnp.int32)], axis=1)
    t, m, *net, up, down, west, east = load(
        t, m, s, k, w1.T, b1.reshape(1, HID), w2, b2, w4, b4.reshape(1, LEV)
    )
    north = lax.ppermute(down, "lat", [(i, i + 1) for i in range(lats - 1)])
    south = lax.ppermute(up, "lat", [(i + 1, i) for i in range(lats - 1)])
    heat_a = some_rows(before_kernel, 2, lit_row, t, m, *net)
    west, east = corners(north, south, west, east)
    from_east = lax.ppermute(west, "lon", [(i, (i - 1) % lons) for i in range(lons)])
    from_west = lax.ppermute(east, "lon", [(i, (i + 1) % lons) for i in range(lons)])
    heat_b = some_rows(after_kernel, 3, lit_row, heat_a, t, m, *net)
    return last(lit_row, t, m, *net, heat_a, heat_b, north, south, west, east, from_west, from_east)


def solution(mesh):
    whole, plane = P(None, "lat", "lon"), P("lat", "lon")
    return jax.shard_map(
        on_device,
        mesh=mesh,
        in_specs=(whole, whole, plane, plane, plane) + (P(),) * 6,
        out_specs=(whole, whole),
        check_vma=False,
    )
```

```python
import functools

import jax
import jax.numpy as jnp
from jax import lax
from jax.experimental import pallas as pl
from jax.experimental.pallas import tpu as pltpu
from jax.sharding import PartitionSpec as P

F32 = jnp.float32
BF16 = jnp.bfloat16
F8 = jnp.float8_e4m3fn

LEV = 90
PAD = 96
ROWS = 32
COLS = 128
HID = 512
FEAT = 181
KIN = 2 * PAD
CHUNK = 8
GROUPS = 4
EARLY = 2
W_LO = 2.0**15
W_HI = 2.0**6
X_LO = 2.0**9
LOAD_LIMIT = 32 << 20

VMEM = pl.BlockSpec(memory_space=pltpu.VMEM)
HBM = pl.BlockSpec(memory_space=pltpu.HBM)


def split(x):
    hi = x.astype(BF16)
    return hi, (x - hi.astype(F32)).astype(BF16)


def lane_index():
    return lax.broadcasted_iota(jnp.int32, (PAD, COLS), 1)


def put_split(hi_ref, eight_ref, w, n):
    hi = w.astype(BF16)
    hi_ref[...] = hi
    eight_ref[:, 0:n] = ((w - hi.astype(F32)) * W_LO).astype(F8)
    eight_ref[:, n : 2 * n] = (w * W_HI).astype(F8)


def column_of(row, n):
    hi = row.astype(BF16)
    rest = row - hi.astype(F32)
    mid = rest.astype(BF16)
    low = (rest - mid.astype(F32)).astype(BF16)
    parts = jnp.concatenate([hi, mid, low, jnp.zeros((13, n), BF16)], axis=0)
    return lax.dot_general(
        parts, jnp.ones((16, COLS), BF16), (((0,), (0,)), ((), ())), preferred_element_type=F32
    )


def power_below(bound):
    scale = jnp.float32(1.0)
    for k in range(9):
        scale = jnp.where(bound > 440.0 * 2.0**k, 0.5 ** (k + 1), scale)
    return scale


def prepare_outer(w1t, b1, b2, w4, b4, w1s, w18, w4s, bs, sc):
    gap = jnp.zeros((PAD - LEV, HID), F32)
    w1 = jnp.concatenate(
        [w1t[0:LEV], gap, w1t[LEV:FEAT], b1[...], gap[0 : PAD - LEV - 2]], axis=0
    )
    put_split(w1s, w18, jnp.transpose(w1 * 0.5), KIN)
    hi, lo = split(jnp.concatenate([w4[...], gap], axis=0))
    w4s[0:PAD] = hi
    w4s[PAD:] = lo
    for k in range(2):
        bs[k * HID : (k + 1) * HID] = column_of(b2[k : k + 1] * 0.5, HID)
    bs[2 * HID : 2 * HID + PAD] = jnp.concatenate(
        [column_of(b4[...], LEV), jnp.zeros((PAD - LEV, COLS), F32)], axis=0
    )
    bound = 6.0 * jnp.max(jnp.sum(jnp.abs(w1), axis=0, keepdims=True))
    put_scale(sc, 0, bound)
    return bound


def put_scale(sc, k, bound):
    scale = power_below(bound)
    sc[k : k + 1] = jnp.full((1, COLS), scale)
    sc[k + 2 : k + 3] = jnp.full((1, COLS), 1.0 / (W_LO * scale))


def prepare_inner(k, w2, w2s, w28):
    put_split(w2s.at[k], w28.at[k], w2[k] * 0.5, HID)


def first_columns(block, r, west, east):
    lane = lane_index()
    place = 2 * (r + 1)
    here = (lane == place) | (lane == place + 1)
    rolled = pltpu.roll(block, place, 1) if place else block
    return jnp.where(here, rolled, west), jnp.where(here, pltpu.roll(block, place + 2, 1), east)


def load_kernel(
    t_hbm, m_hbm, s_hbm, k_hbm, w1_hbm, b1_hbm, w2_hbm, b2_hbm, w4_hbm, b4_hbm,
    t, m, w1s, w18, w2s, w28, w4s, bs, sc, up, down, west_out, east_out,
    k, s, w1, b1, w2, b2, w4, b4, sems,
):
    def rows(src, dst, sem):
        return [pltpu.make_async_copy(src.at[:, r, :], dst.at[r, pl.ds(0, LEV), :], sem) for r in range(ROWS)]

    pairs = ((w1_hbm, w1), (b1_hbm, b1), (b2_hbm, b2), (w4_hbm, w4), (b4_hbm, b4))
    outer = [pltpu.make_async_copy(a, b, sems.at[0]) for a, b in pairs]
    state = [pltpu.make_async_copy(k_hbm, k, sems.at[1])] + rows(t_hbm, t, sems.at[1])
    inner = [pltpu.make_async_copy(w2_hbm.at[i], w2.at[i], sems.at[2 + i]) for i in range(2)]
    humid = [pltpu.make_async_copy(s_hbm, s, sems.at[4])] + rows(m_hbm, m, sems.at[4])
    for copy in outer + state + inner + humid:
        copy.start()
    for copy in outer:
        copy.wait()
    bound = prepare_outer(w1, b1, b2, w4, b4, w1s, w18, w4s, bs, sc)
    for copy in state:
        copy.wait()
    blank = jnp.zeros((PAD - LEV - 1, COLS), F32)
    west = jnp.zeros((PAD, COLS), F32)
    east = jnp.zeros((PAD, COLS), F32)
    for r in range(ROWS):
        t[r, LEV:PAD, :] = jnp.concatenate([k[r : r + 1, :], blank], axis=0)
        west, east = first_columns(t[r], r, west, east)
    west_out[...] = west
    east_out[...] = east
    up[0:PAD] = t[0]
    up[PAD:] = t[1]
    down[0:PAD] = t[ROWS - 1]
    down[PAD:] = t[ROWS - 2]
    inner[0].wait()
    prepare_inner(0, w2, w2s, w28)
    bound = bound * jnp.max(jnp.sum(jnp.abs(w2[0]), axis=1, keepdims=True)) + jnp.max(jnp.abs(b2[...]))
    put_scale(sc, 1, bound)
    inner[1].wait()
    prepare_inner(1, w2, w2s, w28)
    for copy in humid:
        copy.wait()
    one = jnp.ones((1, COLS), F32)
    for r in range(ROWS):
        m[r, LEV:PAD, :] = jnp.concatenate([s[r : r + 1, :], one, blank[1:]], axis=0)


TRACK = jax.ShapeDtypeStruct((ROWS, PAD, COLS), F32)
EDGE = jax.ShapeDtypeStruct((2 * PAD, COLS), F32)
SIDE = jax.ShapeDtypeStruct((PAD, COLS), F32)
WEIGHTS = (
    ((HID, KIN), BF16),
    ((HID, 2 * KIN), F8),
    ((2, HID, HID), BF16),
    ((2, HID, 2 * HID), F8),
    ((2 * PAD, HID), BF16),
    ((2 * HID + PAD, COLS), F32),
    ((8, COLS), F32),
)


def load(*arrays):
    return pl.pallas_call(
        load_kernel,
        out_shape=(TRACK, TRACK)
        + tuple(jax.ShapeDtypeStruct(*w) for w in WEIGHTS)
        + (EDGE, EDGE, SIDE, SIDE),
        in_specs=[HBM] * 10,
        out_specs=(VMEM,) * 13,
        scratch_shapes=[
            pltpu.VMEM((ROWS, COLS), F32),
            pltpu.VMEM((ROWS, COLS), F32),
            pltpu.VMEM((FEAT, HID), F32),
            pltpu.VMEM((1, HID), F32),
            pltpu.VMEM((2, HID, HID), F32),
            pltpu.VMEM((2, HID), F32),
            pltpu.VMEM((LEV, HID), F32),
            pltpu.VMEM((1, LEV), F32),
            pltpu.SemaphoreType.DMA((5,)),
        ],
        compiler_params=pltpu.CompilerParams(vmem_limit_bytes=LOAD_LIMIT),
        cost_estimate=pl.CostEstimate(flops=10**6, bytes_accessed=8 * 10**6, transcendentals=0),
    )(*(pltpu.with_memory_space_constraint(x, pltpu.HBM) for x in arrays))


def corner_kernel(north_ref, south_ref, west_ref, east_ref, w_out, e_out):
    west, east = west_ref[...], east_ref[...]
    west, east = first_columns(north_ref[0:PAD], -1, west, east)
    west, east = first_columns(south_ref[0:PAD], ROWS, west, east)
    w_out[...] = west
    e_out[...] = east


def corners(north, south, west, east):
    side = jax.ShapeDtypeStruct((PAD, COLS), F32)
    return pl.pallas_call(
        corner_kernel,
        out_shape=(side, side),
        in_specs=[VMEM] * 4,
        out_specs=(VMEM, VMEM),
        compiler_params=pltpu.CompilerParams(vmem_limit_bytes=8 << 20),
        cost_estimate=pl.CostEstimate(flops=10**5, bytes_accessed=4 * 10**5, transcendentals=0),
    )(north, south, west, east)


def all_lit(lit_row):
    return jnp.min(lit_row[...].astype(F32)) > 0.5


def lit_rows(lit_ref, info):
    for r in range(ROWS):
        info[r] = 0

    def step(r, carry):
        n, last = carry
        lit = lit_ref[0, r] > 0

        @pl.when(lit)
        def _():
            info[n] = r

        return jnp.where(lit, n + 1, n), jnp.where(lit, r, last)

    n, last = lax.fori_loop(0, ROWS, step, (jnp.int32(0), jnp.int32(0)))

    def fill(i, _):
        info[i] = last
        return 0

    lax.fori_loop(n, ROWS, fill, 0)
    info[ROWS] = n


def count_lit(lit_row, lit_s, info, sem):
    copy = pltpu.make_async_copy(lit_row, lit_s, sem)
    copy.start()
    copy.wait()
    lit_rows(lit_s, info)
    return info[ROWS]


LIST_SCRATCH = [
    pltpu.SMEM((1, COLS), jnp.int32),
    pltpu.SMEM((ROWS + 8,), jnp.int32),
    pltpu.SemaphoreType.DMA,
]


def half_silu(u):
    return u + u * jnp.tanh(u)


def out_layer(w4s, x):
    hi, lo = split(x)
    both = jnp.dot(w4s[...], hi, preferred_element_type=F32)
    return both[0:PAD] + both[PAD:] + jnp.dot(w4s[0:PAD], lo, preferred_element_type=F32)


def parts8(x, scale):
    hi = x.astype(BF16)
    low = x - hi.astype(F32)
    scaled = x if scale is None else x * scale
    factor = X_LO if scale is None else scale * X_LO
    return hi, jnp.concatenate([scaled.astype(F8), (low * factor).astype(F8)], axis=0)


def dot8(w, w8, held, back):
    hi, eight = held
    v = jnp.dot(w, hi, preferred_element_type=F32)
    return v + jnp.dot(w8, eight, preferred_element_type=F32) * back


def network_chunk(rows, t, m, w1s, w18, w2s, w28, w4s, bs, sc, put, between=lambda: None):
    n = CHUNK // GROUPS
    tile = lambda b: jnp.concatenate([b] * n, axis=1)
    scale = [tile(sc[k : k + 1]) for k in range(2)]
    back = [tile(sc[k : k + 1]) for k in range(2, 4)]
    held = [None] * GROUPS
    for g in range(GROUPS):
        x = jnp.concatenate(
            [jnp.concatenate([t[r], m[r]], axis=0) for r in rows[g * n : (g + 1) * n]], axis=1
        )
        v = dot8(w1s[...], w18[...], parts8(x, None), 1.0 / W_LO)
        held[g] = parts8(half_silu(v), scale[0])
        between()
    for k in range(2):
        for g in range(GROUPS):
            v = dot8(w2s[k], w28[k], held[g], back[k])
            h = half_silu(v + tile(bs[k * HID : (k + 1) * HID]))
            held[g] = parts8(h, scale[1]) if k == 0 else h
            between()
    for g in range(GROUPS):
        o = out_layer(w4s, held[g]) + tile(bs[2 * HID : 2 * HID + PAD])
        for j in range(n):
            row = rows[g * n + j]
            put(g * n + j, row, o[:, j * COLS : (j + 1) * COLS] * m[row, LEV : LEV + 1, :])
        between()


def listed(info, c):
    return [info[c * CHUNK + j] for j in range(CHUNK)]


def starts_early():
    return lax.axis_index("lon") < EARLY


def list_or_all(lit_row, lit_s, info, sem):
    every = all_lit(lit_row)

    @pl.when(every)
    def _():
        for r in range(ROWS):
            info[r] = r
        info[ROWS] = ROWS

    @pl.when(jnp.logical_not(every))
    def _():
        count_lit(lit_row, lit_s, info, sem)

    return info[ROWS]


def before_kernel(lit_row, t, m, w1s, w18, w2s, w28, w4s, bs, sc, out, lit_s, info, sem):
    n = list_or_all(lit_row, lit_s, info, sem)
    chunks = jnp.minimum((n + CHUNK - 1) // CHUNK, jnp.where(starts_early(), 2, 1))

    def one(c, _):
        def put(j, row, value):
            out[c * CHUNK + j] = value

        network_chunk(listed(info, c), t, m, w1s, w18, w2s, w28, w4s, bs, sc, put)
        return 0

    lax.fori_loop(0, chunks, one, 0)


def after_kernel(lit_row, before, t, m, w1s, w18, w2s, w28, w4s, bs, sc, out, lit_s, info, sem):
    n = list_or_all(lit_row, lit_s, info, sem)
    early = starts_early()

    @pl.when(early)
    def _():
        out[0:CHUNK] = before[CHUNK : 2 * CHUNK]

    def one(c, _):
        def put(j, row, value):
            out[(c - 1) * CHUNK + j] = value

        network_chunk(listed(info, c), t, m, w1s, w18, w2s, w28, w4s, bs, sc, put)
        return 0

    start = jnp.where(early, 2, 1)
    lax.fori_loop(start, jnp.minimum((n + CHUNK - 1) // CHUNK, start + 2), one, 0)


def some_rows(kernel, blocks, *arrays):
    return pl.pallas_call(
        kernel,
        out_shape=jax.ShapeDtypeStruct((blocks * CHUNK, PAD, COLS), F32),
        in_specs=[VMEM] * len(arrays),
        out_specs=VMEM,
        scratch_shapes=LIST_SCRATCH,
        compiler_params=pltpu.CompilerParams(vmem_limit_bytes=32 << 20),
        cost_estimate=pl.CostEstimate(flops=5 * 10**9, bytes_accessed=8 * 10**6, transcendentals=0),
    )(*arrays)


def last_kernel(
    lit_row, t, m, w1s, w18, w2s, w28, w4s, bs, sc, heat_a, heat_b, north, south, mine_w, mine_e, west, east,
    heat_hbm, temp_hbm, lit_s, info, list_sem, heat_s, step_s, temp_s, sems,
):
    net = (t, m, w1s, w18, w2s, w28, w4s, bs, sc)
    early = starts_early()
    fused = jnp.logical_and(all_lit(lit_row), jnp.logical_not(early))

    def heat_out(r, src=None, at=None):
        src, at = (heat_s, r) if src is None else (src, at)
        return pltpu.make_async_copy(src.at[at, pl.ds(0, LEV), :], heat_hbm.at[:, r, :], sems.at[0])

    def temp_out(r):
        return pltpu.make_async_copy(temp_s.at[r, pl.ds(0, LEV), :], temp_hbm.at[:, r, :], sems.at[1])

    def put(j, row, value):
        heat_s[row] = value

    def state(r):
        if r < 0:
            return north[0:PAD] if r == -1 else north[PAD:]
        if r >= ROWS:
            return south[0:PAD] if r == ROWS else south[PAD:]
        return t[r]

    def number(r):
        if r < 0:
            return north[LEV : LEV + 1]
        if r >= ROWS:
            return south[LEV : LEV + 1]
        return t[r, LEV : LEV + 1, :]

    lane = lane_index()
    odd = lane % 2 == 1
    side = jnp.where(odd, west[...], east[...])

    def compact(far, own, towards):
        near = far[...]
        number = near[LEV : LEV + 1, :]
        around = (
            pltpu.roll(near, 2, 1)
            + pltpu.roll(near, COLS - 2, 1)
            + pltpu.roll(near, towards, 1)
            + pltpu.roll(own[...], towards, 1)
        )
        return near + number * (around - 4.0 * near)

    side_next = jnp.where(odd, compact(west, mine_w, 1), compact(east, mine_e, COLS - 1))
    first_lane, last_lane = lane == 0, lane == COLS - 1

    def substep(above, here, below, number, sides, r):
        edge = pltpu.roll(sides, (-(2 * r + 3)) % COLS, 1)
        left = jnp.where(first_lane, edge, pltpu.roll(here, 1, 1))
        right = jnp.where(last_lane, edge, pltpu.roll(here, COLS - 1, 1))
        return here + number * (above + below + left + right - 4.0 * here)

    def step_one(r):
        step_s[r + 1] = substep(state(r - 1), state(r), state(r + 1), number(r), side, r)

    def step_two(r, heat):
        done = substep(step_s[r], step_s[r + 1], step_s[r + 2], number(r), side_next, r)
        temp_s[r] = done + heat
        temp_out(r).start()

    @pl.when(fused)
    def _():
        def known(r):
            return (heat_a, r) if r < CHUNK else (heat_b, r - CHUNK)

        copies = [heat_out(r, *known(r)) for r in range(3 * CHUNK)]
        for copy in copies:
            copy.start()

        def tasks():
            for r in range(-1, ROWS + 1):
                step_one(r)
                yield
                if 1 <= r <= 3 * CHUNK:
                    block, at = known(r - 1)
                    step_two(r - 1, block[at])
                    yield

        todo = tasks()

        def between():
            for _ in range(4):
                next(todo, None)

        rows = list(range(3 * CHUNK, ROWS))
        network_chunk(rows, *net, put, between)
        for _ in todo:
            pass
        for r in rows:
            copy = heat_out(r)
            copy.start()
            copies.append(copy)
            step_two(r, heat_s[r])
        for copy in copies:
            copy.wait()
        for r in range(ROWS):
            temp_out(r).wait()

    @pl.when(jnp.logical_not(fused))
    def _():
        n = list_or_all(lit_row, lit_s, info, list_sem)
        chunks = (n + CHUNK - 1) // CHUNK

        @pl.when(n < ROWS)
        def _():
            heat_s[...] = jnp.zeros_like(heat_s)

        for part in range(ROWS // CHUNK):
            @pl.when(jnp.logical_and(part < chunks, jnp.logical_or(early, part < 3)))
            def _():
                for j in range(CHUNK):
                    block = heat_a[j] if part == 0 else heat_b[(part - 1) * CHUNK + j]
                    heat_s[info[part * CHUNK + j]] = block

        def one(c, _):
            network_chunk(listed(info, c), *net, put)
            return 0

        lax.fori_loop(jnp.where(early, chunks, 3), chunks, one, 0)
        for r in range(ROWS):
            heat_out(r).start()
        for r in range(-1, ROWS + 1):
            step_one(r)
            if r >= 1:
                step_two(r - 1, heat_s[r - 1])
        for r in range(ROWS):
            heat_out(r).wait()
        for r in range(ROWS):
            temp_out(r).wait()


def last(*arrays):
    whole = jax.ShapeDtypeStruct((LEV, ROWS, COLS), F32)
    track = pltpu.VMEM((ROWS, PAD, COLS), F32)
    return pl.pallas_call(
        last_kernel,
        out_shape=(whole, whole),
        in_specs=[VMEM] * 18,
        out_specs=(HBM, HBM),
        scratch_shapes=LIST_SCRATCH
        + [
            track,
            pltpu.VMEM((ROWS + 2, PAD, COLS), F32),
            track,
            pltpu.SemaphoreType.DMA((2,)),
        ],
        compiler_params=pltpu.CompilerParams(vmem_limit_bytes=32 << 20),
        cost_estimate=pl.CostEstimate(flops=10**10, bytes_accessed=8 * 10**6, transcendentals=0),
    )(*arrays)


def on_device(t, m, s, lit, k, w1, b1, w2, b2, w4, b4):
    lats, lons = lax.axis_size("lat"), lax.axis_size("lon")
    lit_row = jnp.concatenate([lit.reshape(1, ROWS), jnp.ones((1, COLS - ROWS), jnp.int32)], axis=1)
    t, m, *net, up, down, west, east = load(
        t, m, s, k, w1.T, b1.reshape(1, HID), w2, b2, w4, b4.reshape(1, LEV)
    )
    north = lax.ppermute(down, "lat", [(i, i + 1) for i in range(lats - 1)])
    south = lax.ppermute(up, "lat", [(i + 1, i) for i in range(lats - 1)])
    heat_a = some_rows(before_kernel, 2, lit_row, t, m, *net)
    west, east = corners(north, south, west, east)
    from_east = lax.ppermute(west, "lon", [(i, (i - 1) % lons) for i in range(lons)])
    from_west = lax.ppermute(east, "lon", [(i, (i + 1) % lons) for i in range(lons)])
    heat_b = some_rows(after_kernel, 3, lit_row, heat_a, t, m, *net)
    return last(lit_row, t, m, *net, heat_a, heat_b, north, south, west, east, from_west, from_east)


def solution(mesh):
    whole, plane = P(None, "lat", "lon"), P("lat", "lon")
    return jax.shard_map(
        on_device,
        mesh=mesh,
        in_specs=(whole, whole, plane, plane, plane) + (P(),) * 6,
        out_specs=(whole, whole),
        check_vma=False,
    )
```

```python
import functools

import jax
import jax.numpy as jnp
from jax import lax
from jax.experimental import pallas as pl
from jax.experimental.pallas import tpu as pltpu
from jax.sharding import PartitionSpec as P

F32 = jnp.float32
BF16 = jnp.bfloat16
F8 = jnp.float8_e4m3fn

LEV = 90
PAD = 96
ROWS = 32
COLS = 128
HID = 512
FEAT = 181
KIN = 2 * PAD
CHUNK = 8
GROUPS = 4
EARLY = 2
W_LO = 2.0**15
W_HI = 2.0**6
X_LO = 2.0**9
LOAD_LIMIT = 32 << 20

VMEM = pl.BlockSpec(memory_space=pltpu.VMEM)
HBM = pl.BlockSpec(memory_space=pltpu.HBM)


def split(x):
    hi = x.astype(BF16)
    return hi, (x - hi.astype(F32)).astype(BF16)


def lane_index():
    return lax.broadcasted_iota(jnp.int32, (PAD, COLS), 1)


def put_split(hi_ref, eight_ref, w, n):
    hi = w.astype(BF16)
    hi_ref[...] = hi
    eight_ref[:, 0:n] = ((w - hi.astype(F32)) * W_LO).astype(F8)
    eight_ref[:, n : 2 * n] = (w * W_HI).astype(F8)


def column_of(row, n):
    hi = row.astype(BF16)
    rest = row - hi.astype(F32)
    mid = rest.astype(BF16)
    low = (rest - mid.astype(F32)).astype(BF16)
    parts = jnp.concatenate([hi, mid, low, jnp.zeros((13, n), BF16)], axis=0)
    return lax.dot_general(
        parts, jnp.ones((16, COLS), BF16), (((0,), (0,)), ((), ())), preferred_element_type=F32
    )


def power_below(bound):
    scale = jnp.float32(1.0)
    for k in range(9):
        scale = jnp.where(bound > 440.0 * 2.0**k, 0.5 ** (k + 1), scale)
    return scale


def prepare_outer(w1t, b1, b2, w4, b4, w1s, w18, w4s, bs, sc):
    gap = jnp.zeros((PAD - LEV, HID), F32)
    w1 = jnp.concatenate(
        [w1t[0:LEV], gap, w1t[LEV:FEAT], b1[...], gap[0 : PAD - LEV - 2]], axis=0
    )
    put_split(w1s, w18, jnp.transpose(w1 * 0.5), KIN)
    hi, lo = split(jnp.concatenate([w4[...], gap], axis=0))
    w4s[0:PAD] = hi
    w4s[PAD:] = lo
    for k in range(2):
        bs[k * HID : (k + 1) * HID] = column_of(b2[k : k + 1] * 0.5, HID)
    bs[2 * HID : 2 * HID + PAD] = jnp.concatenate(
        [column_of(b4[...], LEV), jnp.zeros((PAD - LEV, COLS), F32)], axis=0
    )
    bound = 6.0 * jnp.max(jnp.sum(jnp.abs(w1), axis=0, keepdims=True))
    put_scale(sc, 0, bound)
    return bound


def put_scale(sc, k, bound):
    scale = power_below(bound)
    sc[k : k + 1] = jnp.full((1, COLS), scale)
    sc[k + 2 : k + 3] = jnp.full((1, COLS), 1.0 / (W_LO * scale))


def prepare_inner(k, w2, w2s, w28):
    put_split(w2s.at[k], w28.at[k], w2[k] * 0.5, HID)


def first_columns(block, r, west, east):
    lane = lane_index()
    place = 2 * (r + 1)
    here = (lane == place) | (lane == place + 1)
    rolled = pltpu.roll(block, place, 1) if place else block
    return jnp.where(here, rolled, west), jnp.where(here, pltpu.roll(block, place + 2, 1), east)


def load_kernel(
    t_hbm, m_hbm, s_hbm, k_hbm, w1_hbm, b1_hbm, w2_hbm, b2_hbm, w4_hbm, b4_hbm,
    t, m, w1s, w18, w2s, w28, w4s, bs, sc, up, down, west_out, east_out,
    k, s, w1, b1, w2, b2, w4, b4, sems,
):
    def rows(src, dst, sem):
        return [pltpu.make_async_copy(src.at[:, r, :], dst.at[r, pl.ds(0, LEV), :], sem) for r in range(ROWS)]

    pairs = ((w1_hbm, w1), (b1_hbm, b1), (b2_hbm, b2), (w4_hbm, w4), (b4_hbm, b4))
    outer = [pltpu.make_async_copy(a, b, sems.at[0]) for a, b in pairs]
    state = [pltpu.make_async_copy(k_hbm, k, sems.at[1])] + rows(t_hbm, t, sems.at[1])
    inner = [pltpu.make_async_copy(w2_hbm.at[i], w2.at[i], sems.at[2 + i]) for i in range(2)]
    humid = [pltpu.make_async_copy(s_hbm, s, sems.at[4])] + rows(m_hbm, m, sems.at[4])
    for copy in outer + state + inner + humid:
        copy.start()
    for copy in outer:
        copy.wait()
    bound = prepare_outer(w1, b1, b2, w4, b4, w1s, w18, w4s, bs, sc)
    for copy in state:
        copy.wait()
    blank = jnp.zeros((PAD - LEV - 1, COLS), F32)
    lane = lane_index()
    west = jnp.zeros((PAD, COLS), F32)
    east = jnp.zeros((PAD, COLS), F32)
    for r in range(ROWS):
        t[r, LEV:PAD, :] = jnp.concatenate([k[r : r + 1, :], blank], axis=0)
        place = 2 * (r + 1)
        rolled = pltpu.roll(t[r], place, 1)
        west = jnp.where((lane == place) | (lane == place + 1), rolled, west)
        east = jnp.where((lane == place - 2) | (lane == place - 1), rolled, east)
    west_out[...] = west
    east_out[...] = pltpu.roll(east, 2, 1)
    up[0:PAD] = t[0]
    up[PAD:] = t[1]
    down[0:PAD] = t[ROWS - 1]
    down[PAD:] = t[ROWS - 2]
    inner[0].wait()
    prepare_inner(0, w2, w2s, w28)
    bound = bound * jnp.max(jnp.sum(jnp.abs(w2[0]), axis=1, keepdims=True)) + jnp.max(jnp.abs(b2[...]))
    put_scale(sc, 1, bound)
    inner[1].wait()
    prepare_inner(1, w2, w2s, w28)
    for copy in humid:
        copy.wait()
    one = jnp.ones((1, COLS), F32)
    for r in range(ROWS):
        m[r, LEV:PAD, :] = jnp.concatenate([s[r : r + 1, :], one, blank[1:]], axis=0)


TRACK = jax.ShapeDtypeStruct((ROWS, PAD, COLS), F32)
EDGE = jax.ShapeDtypeStruct((2 * PAD, COLS), F32)
SIDE = jax.ShapeDtypeStruct((PAD, COLS), F32)
WEIGHTS = (
    ((HID, KIN), BF16),
    ((HID, 2 * KIN), F8),
    ((2, HID, HID), BF16),
    ((2, HID, 2 * HID), F8),
    ((2 * PAD, HID), BF16),
    ((2 * HID + PAD, COLS), F32),
    ((8, COLS), F32),
)


def load(*arrays):
    return pl.pallas_call(
        load_kernel,
        out_shape=(TRACK, TRACK)
        + tuple(jax.ShapeDtypeStruct(*w) for w in WEIGHTS)
        + (EDGE, EDGE, SIDE, SIDE),
        in_specs=[HBM] * 10,
        out_specs=(VMEM,) * 13,
        scratch_shapes=[
            pltpu.VMEM((ROWS, COLS), F32),
            pltpu.VMEM((ROWS, COLS), F32),
            pltpu.VMEM((FEAT, HID), F32),
            pltpu.VMEM((1, HID), F32),
            pltpu.VMEM((2, HID, HID), F32),
            pltpu.VMEM((2, HID), F32),
            pltpu.VMEM((LEV, HID), F32),
            pltpu.VMEM((1, LEV), F32),
            pltpu.SemaphoreType.DMA((5,)),
        ],
        compiler_params=pltpu.CompilerParams(vmem_limit_bytes=LOAD_LIMIT),
        cost_estimate=pl.CostEstimate(flops=10**6, bytes_accessed=8 * 10**6, transcendentals=0),
    )(*(pltpu.with_memory_space_constraint(x, pltpu.HBM) for x in arrays))


def corner_kernel(north_ref, south_ref, west_ref, east_ref, w_out, e_out):
    west, east = west_ref[...], east_ref[...]
    west, east = first_columns(north_ref[0:PAD], -1, west, east)
    west, east = first_columns(south_ref[0:PAD], ROWS, west, east)
    w_out[...] = west
    e_out[...] = east


def corners(north, south, west, east):
    side = jax.ShapeDtypeStruct((PAD, COLS), F32)
    return pl.pallas_call(
        corner_kernel,
        out_shape=(side, side),
        in_specs=[VMEM] * 4,
        out_specs=(VMEM, VMEM),
        compiler_params=pltpu.CompilerParams(vmem_limit_bytes=8 << 20),
        cost_estimate=pl.CostEstimate(flops=10**5, bytes_accessed=4 * 10**5, transcendentals=0),
    )(north, south, west, east)


def all_lit(lit_row):
    return jnp.min(lit_row[...].astype(F32)) > 0.5


def lit_rows(lit_ref, info):
    for r in range(ROWS):
        info[r] = 0

    def step(r, carry):
        n, last = carry
        lit = lit_ref[0, r] > 0

        @pl.when(lit)
        def _():
            info[n] = r

        return jnp.where(lit, n + 1, n), jnp.where(lit, r, last)

    n, last = lax.fori_loop(0, ROWS, step, (jnp.int32(0), jnp.int32(0)))

    def fill(i, _):
        info[i] = last
        return 0

    lax.fori_loop(n, ROWS, fill, 0)
    info[ROWS] = n


def count_lit(lit_row, lit_s, info, sem):
    copy = pltpu.make_async_copy(lit_row, lit_s, sem)
    copy.start()
    copy.wait()
    lit_rows(lit_s, info)
    return info[ROWS]


LIST_SCRATCH = [
    pltpu.SMEM((1, COLS), jnp.int32),
    pltpu.SMEM((ROWS + 8,), jnp.int32),
    pltpu.SemaphoreType.DMA,
]


def half_silu(u):
    return u + u * jnp.tanh(u)


def out_layer(w4s, x):
    hi, lo = split(x)
    both = jnp.dot(w4s[...], hi, preferred_element_type=F32)
    return both[0:PAD] + both[PAD:] + jnp.dot(w4s[0:PAD], lo, preferred_element_type=F32)


def parts8(x, scale):
    hi = x.astype(BF16)
    low = x - hi.astype(F32)
    scaled = x if scale is None else x * scale
    factor = X_LO if scale is None else scale * X_LO
    return hi, jnp.concatenate([scaled.astype(F8), (low * factor).astype(F8)], axis=0)


def dot8(w, w8, held, back):
    hi, eight = held
    v = jnp.dot(w, hi, preferred_element_type=F32)
    return v + jnp.dot(w8, eight, preferred_element_type=F32) * back


def network_chunk(rows, t, m, w1s, w18, w2s, w28, w4s, bs, sc, put, between=lambda: None):
    n = CHUNK // GROUPS
    tile = lambda b: jnp.concatenate([b] * n, axis=1)
    scale = [tile(sc[k : k + 1]) for k in range(2)]
    back = [tile(sc[k : k + 1]) for k in range(2, 4)]
    held = [None] * GROUPS
    for g in range(GROUPS):
        x = jnp.concatenate(
            [jnp.concatenate([t[r], m[r]], axis=0) for r in rows[g * n : (g + 1) * n]], axis=1
        )
        v = dot8(w1s[...], w18[...], parts8(x, None), 1.0 / W_LO)
        held[g] = parts8(half_silu(v), scale[0])
        between()
    for k in range(2):
        for g in range(GROUPS):
            v = dot8(w2s[k], w28[k], held[g], back[k])
            h = half_silu(v + tile(bs[k * HID : (k + 1) * HID]))
            held[g] = parts8(h, scale[1]) if k == 0 else h
            between()
    for g in range(GROUPS):
        o = out_layer(w4s, held[g]) + tile(bs[2 * HID : 2 * HID + PAD])
        for j in range(n):
            row = rows[g * n + j]
            put(g * n + j, row, o[:, j * COLS : (j + 1) * COLS] * m[row, LEV : LEV + 1, :])
        between()


def listed(info, c):
    return [info[c * CHUNK + j] for j in range(CHUNK)]


def starts_early():
    return lax.axis_index("lon") < EARLY


def list_or_all(lit_row, lit_s, info, sem):
    every = all_lit(lit_row)

    @pl.when(every)
    def _():
        for r in range(ROWS):
            info[r] = r
        info[ROWS] = ROWS

    @pl.when(jnp.logical_not(every))
    def _():
        count_lit(lit_row, lit_s, info, sem)

    return info[ROWS]


def before_kernel(lit_row, t, m, w1s, w18, w2s, w28, w4s, bs, sc, out, lit_s, info, sem):
    n = list_or_all(lit_row, lit_s, info, sem)
    chunks = jnp.minimum((n + CHUNK - 1) // CHUNK, jnp.where(starts_early(), 2, 1))

    def one(c, _):
        def put(j, row, value):
            out[c * CHUNK + j] = value

        network_chunk(listed(info, c), t, m, w1s, w18, w2s, w28, w4s, bs, sc, put)
        return 0

    lax.fori_loop(0, chunks, one, 0)


def after_kernel(lit_row, before, t, m, w1s, w18, w2s, w28, w4s, bs, sc, out, lit_s, info, sem):
    n = list_or_all(lit_row, lit_s, info, sem)
    early = starts_early()

    @pl.when(early)
    def _():
        out[0:CHUNK] = before[CHUNK : 2 * CHUNK]

    def one(c, _):
        def put(j, row, value):
            out[(c - 1) * CHUNK + j] = value

        network_chunk(listed(info, c), t, m, w1s, w18, w2s, w28, w4s, bs, sc, put)
        return 0

    start = jnp.where(early, 2, 1)
    lax.fori_loop(start, jnp.minimum((n + CHUNK - 1) // CHUNK, start + 2), one, 0)


def some_rows(kernel, blocks, *arrays):
    return pl.pallas_call(
        kernel,
        out_shape=jax.ShapeDtypeStruct((blocks * CHUNK, PAD, COLS), F32),
        in_specs=[VMEM] * len(arrays),
        out_specs=VMEM,
        scratch_shapes=LIST_SCRATCH,
        compiler_params=pltpu.CompilerParams(vmem_limit_bytes=32 << 20),
        cost_estimate=pl.CostEstimate(flops=5 * 10**9, bytes_accessed=8 * 10**6, transcendentals=0),
    )(*arrays)


def last_kernel(
    lit_row, t, m, w1s, w18, w2s, w28, w4s, bs, sc, heat_a, heat_b, north, south, mine_w, mine_e, west, east,
    heat_hbm, temp_hbm, lit_s, info, list_sem, heat_s, step_s, temp_s, sems,
):
    net = (t, m, w1s, w18, w2s, w28, w4s, bs, sc)
    early = starts_early()
    every = all_lit(lit_row)

    def heat_out(r, src=None, at=None):
        src, at = (heat_s, r) if src is None else (src, at)
        return pltpu.make_async_copy(src.at[at, pl.ds(0, LEV), :], heat_hbm.at[:, r, :], sems.at[0])

    def temp_out(r):
        return pltpu.make_async_copy(temp_s.at[r, pl.ds(0, LEV), :], temp_hbm.at[:, r, :], sems.at[1])

    def put(j, row, value):
        heat_s[row] = value

    def state(r):
        if r < 0:
            return north[0:PAD] if r == -1 else north[PAD:]
        if r >= ROWS:
            return south[0:PAD] if r == ROWS else south[PAD:]
        return t[r]

    def number(r):
        if r < 0:
            return north[LEV : LEV + 1]
        if r >= ROWS:
            return south[LEV : LEV + 1]
        return t[r, LEV : LEV + 1, :]

    lane = lane_index()
    odd = lane % 2 == 1
    side = jnp.where(odd, west[...], east[...])

    def compact(far, own, towards):
        near = far[...]
        number = near[LEV : LEV + 1, :]
        around = (
            pltpu.roll(near, 2, 1)
            + pltpu.roll(near, COLS - 2, 1)
            + pltpu.roll(near, towards, 1)
            + pltpu.roll(own[...], towards, 1)
        )
        return near + number * (around - 4.0 * near)

    side_next = jnp.where(odd, compact(west, mine_w, 1), compact(east, mine_e, COLS - 1))
    first_lane, last_lane = lane == 0, lane == COLS - 1

    def substep(above, here, below, number, sides, r):
        edge = pltpu.roll(sides, (-(2 * r + 3)) % COLS, 1)
        left = jnp.where(first_lane, edge, pltpu.roll(here, 1, 1))
        right = jnp.where(last_lane, edge, pltpu.roll(here, COLS - 1, 1))
        return here + number * (above + below + left + right - 4.0 * here)

    def step_one(r):
        step_s[r + 1] = substep(state(r - 1), state(r), state(r + 1), number(r), side, r)

    def step_two(r, heat):
        done = substep(step_s[r], step_s[r + 1], step_s[r + 2], number(r), side_next, r)
        temp_s[r] = done + heat
        temp_out(r).start()

    def known(r):
        return (heat_a, r) if r < CHUNK else (heat_b, r - CHUNK)

    def tasks(count):
        for r in range(-1, ROWS + 1):
            step_one(r)
            yield
            if 1 <= r <= count:
                block, at = known(r - 1)
                step_two(r - 1, block[at])
                yield

    @pl.when(jnp.logical_and(every, early))
    def _():
        copies = [heat_out(r, *known(r)) for r in range(ROWS)]
        for copy in copies:
            copy.start()
        for _ in tasks(ROWS):
            pass
        for copy in copies:
            copy.wait()
        for r in range(ROWS):
            temp_out(r).wait()

    @pl.when(jnp.logical_and(every, jnp.logical_not(early)))
    def _():
        copies = [heat_out(r, *known(r)) for r in range(3 * CHUNK)]
        for copy in copies:
            copy.start()
        todo = tasks(3 * CHUNK)

        def between():
            for _ in range(4):
                next(todo, None)

        rows = list(range(3 * CHUNK, ROWS))
        network_chunk(rows, *net, put, between)
        for _ in todo:
            pass
        for r in rows:
            copy = heat_out(r)
            copy.start()
            copies.append(copy)
            step_two(r, heat_s[r])
        for copy in copies:
            copy.wait()
        for r in range(ROWS):
            temp_out(r).wait()

    @pl.when(jnp.logical_not(every))
    def _():
        n = count_lit(lit_row, lit_s, info, list_sem)
        chunks = (n + CHUNK - 1) // CHUNK

        heat_s[...] = jnp.zeros_like(heat_s)
        for part in range(ROWS // CHUNK):
            @pl.when(jnp.logical_and(part < chunks, jnp.logical_or(early, part < 3)))
            def _():
                for j in range(CHUNK):
                    block = heat_a[j] if part == 0 else heat_b[(part - 1) * CHUNK + j]
                    heat_s[info[part * CHUNK + j]] = block

        def one(c, _):
            network_chunk(listed(info, c), *net, put)
            return 0

        lax.fori_loop(jnp.where(early, chunks, 3), chunks, one, 0)
        for r in range(ROWS):
            heat_out(r).start()
        for r in range(-1, ROWS + 1):
            step_one(r)
            if r >= 1:
                step_two(r - 1, heat_s[r - 1])
        for r in range(ROWS):
            heat_out(r).wait()
        for r in range(ROWS):
            temp_out(r).wait()


def last(*arrays):
    whole = jax.ShapeDtypeStruct((LEV, ROWS, COLS), F32)
    track = pltpu.VMEM((ROWS, PAD, COLS), F32)
    return pl.pallas_call(
        last_kernel,
        out_shape=(whole, whole),
        in_specs=[VMEM] * 18,
        out_specs=(HBM, HBM),
        scratch_shapes=LIST_SCRATCH
        + [
            track,
            pltpu.VMEM((ROWS + 2, PAD, COLS), F32),
            track,
            pltpu.SemaphoreType.DMA((2,)),
        ],
        compiler_params=pltpu.CompilerParams(vmem_limit_bytes=32 << 20),
        cost_estimate=pl.CostEstimate(flops=10**10, bytes_accessed=8 * 10**6, transcendentals=0),
    )(*arrays)


def on_device(t, m, s, lit, k, w1, b1, w2, b2, w4, b4):
    lats, lons = lax.axis_size("lat"), lax.axis_size("lon")
    lit_row = jnp.concatenate([lit.reshape(1, ROWS), jnp.ones((1, COLS - ROWS), jnp.int32)], axis=1)
    t, m, *net, up, down, west, east = load(
        t, m, s, k, w1.T, b1.reshape(1, HID), w2, b2, w4, b4.reshape(1, LEV)
    )
    north = lax.ppermute(down, "lat", [(i, i + 1) for i in range(lats - 1)])
    south = lax.ppermute(up, "lat", [(i + 1, i) for i in range(lats - 1)])
    heat_a = some_rows(before_kernel, 2, lit_row, t, m, *net)
    west, east = corners(north, south, west, east)
    from_east = lax.ppermute(west, "lon", [(i, (i - 1) % lons) for i in range(lons)])
    from_west = lax.ppermute(east, "lon", [(i, (i + 1) % lons) for i in range(lons)])
    heat_b = some_rows(after_kernel, 3, lit_row, heat_a, t, m, *net)
    return last(lit_row, t, m, *net, heat_a, heat_b, north, south, west, east, from_west, from_east)


def solution(mesh):
    whole, plane = P(None, "lat", "lon"), P("lat", "lon")
    return jax.shard_map(
        on_device,
        mesh=mesh,
        in_specs=(whole, whole, plane, plane, plane) + (P(),) * 6,
        out_specs=(whole, whole),
        check_vma=False,
    )
```

```python
import functools

import jax
import jax.numpy as jnp
from jax import lax
from jax.experimental import pallas as pl
from jax.experimental.pallas import tpu as pltpu
from jax.sharding import PartitionSpec as P

F32 = jnp.float32
BF16 = jnp.bfloat16
F8 = jnp.float8_e4m3fn

LEV = 90
PAD = 96
ROWS = 32
COLS = 128
HID = 512
FEAT = 181
KIN = 2 * PAD
CHUNK = 8
GROUPS = 4
EARLY = 2
W_LO = 2.0**15
W_HI = 2.0**6
X_LO = 2.0**9
LOAD_LIMIT = 32 << 20

VMEM = pl.BlockSpec(memory_space=pltpu.VMEM)
HBM = pl.BlockSpec(memory_space=pltpu.HBM)


def split(x):
    hi = x.astype(BF16)
    return hi, (x - hi.astype(F32)).astype(BF16)


def lane_index():
    return lax.broadcasted_iota(jnp.int32, (PAD, COLS), 1)


def put_split(hi_ref, eight_ref, w, n):
    hi = w.astype(BF16)
    hi_ref[...] = hi
    eight_ref[:, 0:n] = ((w - hi.astype(F32)) * W_LO).astype(F8)
    eight_ref[:, n : 2 * n] = (w * W_HI).astype(F8)


def column_of(row, n):
    hi = row.astype(BF16)
    rest = row - hi.astype(F32)
    mid = rest.astype(BF16)
    low = (rest - mid.astype(F32)).astype(BF16)
    parts = jnp.concatenate([hi, mid, low, jnp.zeros((13, n), BF16)], axis=0)
    return lax.dot_general(
        parts, jnp.ones((16, COLS), BF16), (((0,), (0,)), ((), ())), preferred_element_type=F32
    )


def power_below(bound):
    scale = jnp.float32(1.0)
    for k in range(9):
        scale = jnp.where(bound > 440.0 * 2.0**k, 0.5 ** (k + 1), scale)
    return scale


def prepare_outer(w1t, b1, b2, w4, b4, w1s, w18, w4s, bs, sc):
    gap = jnp.zeros((PAD - LEV, HID), F32)
    w1 = jnp.concatenate(
        [w1t[0:LEV], gap, w1t[LEV:FEAT], b1[...], gap[0 : PAD - LEV - 2]], axis=0
    )
    put_split(w1s, w18, jnp.transpose(w1 * 0.5), KIN)
    hi, lo = split(jnp.concatenate([w4[...], gap], axis=0))
    w4s[0:PAD] = hi
    w4s[PAD:] = lo
    for k in range(2):
        bs[k * HID : (k + 1) * HID] = column_of(b2[k : k + 1] * 0.5, HID)
    bs[2 * HID : 2 * HID + PAD] = jnp.concatenate(
        [column_of(b4[...], LEV), jnp.zeros((PAD - LEV, COLS), F32)], axis=0
    )
    bound = 6.0 * jnp.max(jnp.sum(jnp.abs(w1), axis=0, keepdims=True))
    put_scale(sc, 0, bound)
    return bound


def put_scale(sc, k, bound):
    scale = power_below(bound)
    sc[k : k + 1] = jnp.full((1, COLS), scale)
    sc[k + 2 : k + 3] = jnp.full((1, COLS), 1.0 / (W_LO * scale))


def prepare_inner(k, w2, w2s, w28):
    put_split(w2s.at[k], w28.at[k], w2[k] * 0.5, HID)


def first_columns(block, r, west, east):
    lane = lane_index()
    place = 2 * (r + 1)
    here = (lane == place) | (lane == place + 1)
    rolled = pltpu.roll(block, place, 1) if place else block
    return jnp.where(here, rolled, west), jnp.where(here, pltpu.roll(block, place + 2, 1), east)


def load_kernel(
    t_hbm, m_hbm, s_hbm, k_hbm, w1_hbm, b1_hbm, w2_hbm, b2_hbm, w4_hbm, b4_hbm,
    t, m, w1s, w18, w2s, w28, w4s, bs, sc, up, down, west_out, east_out,
    k, s, w1, b1, w2, b2, w4, b4, sems,
):
    def rows(src, dst, sem):
        return [pltpu.make_async_copy(src.at[:, r, :], dst.at[r, pl.ds(0, LEV), :], sem) for r in range(ROWS)]

    pairs = ((w1_hbm, w1), (b1_hbm, b1), (b2_hbm, b2), (w4_hbm, w4), (b4_hbm, b4))
    outer = [pltpu.make_async_copy(a, b, sems.at[0]) for a, b in pairs]
    state = [pltpu.make_async_copy(k_hbm, k, sems.at[1])] + rows(t_hbm, t, sems.at[1])
    inner = [pltpu.make_async_copy(w2_hbm.at[i], w2.at[i], sems.at[2 + i]) for i in range(2)]
    humid = [pltpu.make_async_copy(s_hbm, s, sems.at[4])] + rows(m_hbm, m, sems.at[4])
    for copy in outer + inner + state + humid:
        copy.start()
    for copy in outer:
        copy.wait()
    bound = prepare_outer(w1, b1, b2, w4, b4, w1s, w18, w4s, bs, sc)
    inner[0].wait()
    prepare_inner(0, w2, w2s, w28)
    bound = bound * jnp.max(jnp.sum(jnp.abs(w2[0]), axis=1, keepdims=True)) + jnp.max(jnp.abs(b2[...]))
    put_scale(sc, 1, bound)
    inner[1].wait()
    prepare_inner(1, w2, w2s, w28)
    for copy in state:
        copy.wait()
    blank = jnp.zeros((PAD - LEV - 1, COLS), F32)
    lane = lane_index()
    west = jnp.zeros((PAD, COLS), F32)
    east = jnp.zeros((PAD, COLS), F32)
    for r in range(ROWS):
        t[r, LEV:PAD, :] = jnp.concatenate([k[r : r + 1, :], blank], axis=0)
        place = 2 * (r + 1)
        rolled = pltpu.roll(t[r], place, 1)
        west = jnp.where((lane == place) | (lane == place + 1), rolled, west)
        east = jnp.where((lane == place - 2) | (lane == place - 1), rolled, east)
    west_out[...] = west
    east_out[...] = pltpu.roll(east, 2, 1)
    up[0:PAD] = t[0]
    up[PAD:] = t[1]
    down[0:PAD] = t[ROWS - 1]
    down[PAD:] = t[ROWS - 2]
    for copy in humid:
        copy.wait()
    one = jnp.ones((1, COLS), F32)
    for r in range(ROWS):
        m[r, LEV:PAD, :] = jnp.concatenate([s[r : r + 1, :], one, blank[1:]], axis=0)


TRACK = jax.ShapeDtypeStruct((ROWS, PAD, COLS), F32)
EDGE = jax.ShapeDtypeStruct((2 * PAD, COLS), F32)
SIDE = jax.ShapeDtypeStruct((PAD, COLS), F32)
WEIGHTS = (
    ((HID, KIN), BF16),
    ((HID, 2 * KIN), F8),
    ((2, HID, HID), BF16),
    ((2, HID, 2 * HID), F8),
    ((2 * PAD, HID), BF16),
    ((2 * HID + PAD, COLS), F32),
    ((8, COLS), F32),
)


def load(*arrays):
    return pl.pallas_call(
        load_kernel,
        out_shape=(TRACK, TRACK)
        + tuple(jax.ShapeDtypeStruct(*w) for w in WEIGHTS)
        + (EDGE, EDGE, SIDE, SIDE),
        in_specs=[HBM] * 10,
        out_specs=(VMEM,) * 13,
        scratch_shapes=[
            pltpu.VMEM((ROWS, COLS), F32),
            pltpu.VMEM((ROWS, COLS), F32),
            pltpu.VMEM((FEAT, HID), F32),
            pltpu.VMEM((1, HID), F32),
            pltpu.VMEM((2, HID, HID), F32),
            pltpu.VMEM((2, HID), F32),
            pltpu.VMEM((LEV, HID), F32),
            pltpu.VMEM((1, LEV), F32),
            pltpu.SemaphoreType.DMA((5,)),
        ],
        compiler_params=pltpu.CompilerParams(vmem_limit_bytes=LOAD_LIMIT),
        cost_estimate=pl.CostEstimate(flops=10**6, bytes_accessed=8 * 10**6, transcendentals=0),
    )(*(pltpu.with_memory_space_constraint(x, pltpu.HBM) for x in arrays))


def corner_kernel(north_ref, south_ref, west_ref, east_ref, w_out, e_out):
    west, east = west_ref[...], east_ref[...]
    west, east = first_columns(north_ref[0:PAD], -1, west, east)
    west, east = first_columns(south_ref[0:PAD], ROWS, west, east)
    w_out[...] = west
    e_out[...] = east


def corners(north, south, west, east):
    side = jax.ShapeDtypeStruct((PAD, COLS), F32)
    return pl.pallas_call(
        corner_kernel,
        out_shape=(side, side),
        in_specs=[VMEM] * 4,
        out_specs=(VMEM, VMEM),
        compiler_params=pltpu.CompilerParams(vmem_limit_bytes=8 << 20),
        cost_estimate=pl.CostEstimate(flops=10**5, bytes_accessed=4 * 10**5, transcendentals=0),
    )(north, south, west, east)


def all_lit(lit_row):
    return jnp.min(lit_row[...].astype(F32)) > 0.5


def lit_rows(lit_ref, info):
    for r in range(ROWS):
        info[r] = 0

    def step(r, carry):
        n, last = carry
        lit = lit_ref[0, r] > 0

        @pl.when(lit)
        def _():
            info[n] = r

        return jnp.where(lit, n + 1, n), jnp.where(lit, r, last)

    n, last = lax.fori_loop(0, ROWS, step, (jnp.int32(0), jnp.int32(0)))

    def fill(i, _):
        info[i] = last
        return 0

    lax.fori_loop(n, ROWS, fill, 0)
    info[ROWS] = n


def count_lit(lit_row, lit_s, info, sem):
    copy = pltpu.make_async_copy(lit_row, lit_s, sem)
    copy.start()
    copy.wait()
    lit_rows(lit_s, info)
    return info[ROWS]


LIST_SCRATCH = [
    pltpu.SMEM((1, COLS), jnp.int32),
    pltpu.SMEM((ROWS + 8,), jnp.int32),
    pltpu.SemaphoreType.DMA,
]


def half_silu(u):
    return u + u * jnp.tanh(u)


def out_layer(w4s, x):
    hi, lo = split(x)
    both = jnp.dot(w4s[...], hi, preferred_element_type=F32)
    return both[0:PAD] + both[PAD:] + jnp.dot(w4s[0:PAD], lo, preferred_element_type=F32)


def parts8(x, scale):
    hi = x.astype(BF16)
    low = x - hi.astype(F32)
    scaled = x if scale is None else x * scale
    factor = X_LO if scale is None else scale * X_LO
    return hi, jnp.concatenate([scaled.astype(F8), (low * factor).astype(F8)], axis=0)


def dot8(w, w8, held, back):
    hi, eight = held
    v = jnp.dot(w, hi, preferred_element_type=F32)
    return v + jnp.dot(w8, eight, preferred_element_type=F32) * back


def network_chunk(rows, t, m, w1s, w18, w2s, w28, w4s, bs, sc, put, between=lambda: None):
    n = CHUNK // GROUPS
    tile = lambda b: jnp.concatenate([b] * n, axis=1)
    scale = [tile(sc[k : k + 1]) for k in range(2)]
    back = [tile(sc[k : k + 1]) for k in range(2, 4)]
    held = [None] * GROUPS
    for g in range(GROUPS):
        x = jnp.concatenate(
            [jnp.concatenate([t[r], m[r]], axis=0) for r in rows[g * n : (g + 1) * n]], axis=1
        )
        v = dot8(w1s[...], w18[...], parts8(x, None), 1.0 / W_LO)
        held[g] = parts8(half_silu(v), scale[0])
        between()
    for k in range(2):
        for g in range(GROUPS):
            v = dot8(w2s[k], w28[k], held[g], back[k])
            h = half_silu(v + tile(bs[k * HID : (k + 1) * HID]))
            held[g] = parts8(h, scale[1]) if k == 0 else h
            between()
    for g in range(GROUPS):
        o = out_layer(w4s, held[g]) + tile(bs[2 * HID : 2 * HID + PAD])
        for j in range(n):
            row = rows[g * n + j]
            put(g * n + j, row, o[:, j * COLS : (j + 1) * COLS] * m[row, LEV : LEV + 1, :])
        between()


def listed(info, c):
    return [info[c * CHUNK + j] for j in range(CHUNK)]


def starts_early():
    return lax.axis_index("lon") < EARLY


def list_or_all(lit_row, lit_s, info, sem):
    every = all_lit(lit_row)

    @pl.when(every)
    def _():
        for r in range(ROWS):
            info[r] = r
        info[ROWS] = ROWS

    @pl.when(jnp.logical_not(every))
    def _():
        count_lit(lit_row, lit_s, info, sem)

    return info[ROWS]


def before_kernel(lit_row, t, m, w1s, w18, w2s, w28, w4s, bs, sc, out, lit_s, info, sem):
    n = list_or_all(lit_row, lit_s, info, sem)
    chunks = jnp.minimum((n + CHUNK - 1) // CHUNK, jnp.where(starts_early(), 2, 1))

    def one(c, _):
        def put(j, row, value):
            out[c * CHUNK + j] = value

        network_chunk(listed(info, c), t, m, w1s, w18, w2s, w28, w4s, bs, sc, put)
        return 0

    lax.fori_loop(0, chunks, one, 0)


def after_kernel(lit_row, before, t, m, w1s, w18, w2s, w28, w4s, bs, sc, out, lit_s, info, sem):
    n = list_or_all(lit_row, lit_s, info, sem)
    early = starts_early()

    @pl.when(early)
    def _():
        out[0:CHUNK] = before[CHUNK : 2 * CHUNK]

    def one(c, _):
        def put(j, row, value):
            out[(c - 1) * CHUNK + j] = value

        network_chunk(listed(info, c), t, m, w1s, w18, w2s, w28, w4s, bs, sc, put)
        return 0

    start = jnp.where(early, 2, 1)
    lax.fori_loop(start, jnp.minimum((n + CHUNK - 1) // CHUNK, start + 2), one, 0)


def some_rows(kernel, blocks, *arrays):
    return pl.pallas_call(
        kernel,
        out_shape=jax.ShapeDtypeStruct((blocks * CHUNK, PAD, COLS), F32),
        in_specs=[VMEM] * len(arrays),
        out_specs=VMEM,
        scratch_shapes=LIST_SCRATCH,
        compiler_params=pltpu.CompilerParams(vmem_limit_bytes=32 << 20),
        cost_estimate=pl.CostEstimate(flops=5 * 10**9, bytes_accessed=8 * 10**6, transcendentals=0),
    )(*arrays)


def last_kernel(
    lit_row, t, m, w1s, w18, w2s, w28, w4s, bs, sc, heat_a, heat_b, north, south, mine_w, mine_e, west, east,
    heat_hbm, temp_hbm, lit_s, info, list_sem, heat_s, step_s, temp_s, sems,
):
    net = (t, m, w1s, w18, w2s, w28, w4s, bs, sc)
    early = starts_early()
    every = all_lit(lit_row)

    def heat_out(r, src=None, at=None):
        src, at = (heat_s, r) if src is None else (src, at)
        return pltpu.make_async_copy(src.at[at, pl.ds(0, LEV), :], heat_hbm.at[:, r, :], sems.at[0])

    def temp_out(r):
        return pltpu.make_async_copy(temp_s.at[r, pl.ds(0, LEV), :], temp_hbm.at[:, r, :], sems.at[1])

    def put(j, row, value):
        heat_s[row] = value

    def state(r):
        if r < 0:
            return north[0:PAD] if r == -1 else north[PAD:]
        if r >= ROWS:
            return south[0:PAD] if r == ROWS else south[PAD:]
        return t[r]

    def number(r):
        if r < 0:
            return north[LEV : LEV + 1]
        if r >= ROWS:
            return south[LEV : LEV + 1]
        return t[r, LEV : LEV + 1, :]

    lane = lane_index()
    odd = lane % 2 == 1
    side = jnp.where(odd, west[...], east[...])

    def compact(far, own, towards):
        near = far[...]
        number = near[LEV : LEV + 1, :]
        around = (
            pltpu.roll(near, 2, 1)
            + pltpu.roll(near, COLS - 2, 1)
            + pltpu.roll(near, towards, 1)
            + pltpu.roll(own[...], towards, 1)
        )
        return near + number * (around - 4.0 * near)

    side_next = jnp.where(odd, compact(west, mine_w, 1), compact(east, mine_e, COLS - 1))
    first_lane, last_lane = lane == 0, lane == COLS - 1

    def substep(above, here, below, number, sides, r):
        edge = pltpu.roll(sides, (-(2 * r + 3)) % COLS, 1)
        left = jnp.where(first_lane, edge, pltpu.roll(here, 1, 1))
        right = jnp.where(last_lane, edge, pltpu.roll(here, COLS - 1, 1))
        return here + number * (above + below + left + right - 4.0 * here)

    def step_one(r):
        step_s[r + 1] = substep(state(r - 1), state(r), state(r + 1), number(r), side, r)

    def step_two(r, heat):
        done = substep(step_s[r], step_s[r + 1], step_s[r + 2], number(r), side_next, r)
        temp_s[r] = done + heat
        temp_out(r).start()

    def known(r):
        return (heat_a, r) if r < CHUNK else (heat_b, r - CHUNK)

    def tasks(count):
        for r in range(-1, ROWS + 1):
            step_one(r)
            yield
            if 1 <= r <= count:
                block, at = known(r - 1)
                step_two(r - 1, block[at])
                yield

    @pl.when(jnp.logical_and(every, early))
    def _():
        copies = [heat_out(r, *known(r)) for r in range(ROWS)]
        for copy in copies:
            copy.start()
        for _ in tasks(ROWS):
            pass
        for copy in copies:
            copy.wait()
        for r in range(ROWS):
            temp_out(r).wait()

    @pl.when(jnp.logical_and(every, jnp.logical_not(early)))
    def _():
        copies = [heat_out(r, *known(r)) for r in range(3 * CHUNK)]
        for copy in copies:
            copy.start()
        todo = tasks(3 * CHUNK)

        def between():
            for _ in range(4):
                next(todo, None)

        rows = list(range(3 * CHUNK, ROWS))
        network_chunk(rows, *net, put, between)
        for _ in todo:
            pass
        for r in rows:
            copy = heat_out(r)
            copy.start()
            copies.append(copy)
            step_two(r, heat_s[r])
        for copy in copies:
            copy.wait()
        for r in range(ROWS):
            temp_out(r).wait()

    @pl.when(jnp.logical_not(every))
    def _():
        n = count_lit(lit_row, lit_s, info, list_sem)
        chunks = (n + CHUNK - 1) // CHUNK

        heat_s[...] = jnp.zeros_like(heat_s)
        for part in range(ROWS // CHUNK):
            @pl.when(jnp.logical_and(part < chunks, jnp.logical_or(early, part < 3)))
            def _():
                for j in range(CHUNK):
                    block = heat_a[j] if part == 0 else heat_b[(part - 1) * CHUNK + j]
                    heat_s[info[part * CHUNK + j]] = block

        def one(c, _):
            network_chunk(listed(info, c), *net, put)
            return 0

        lax.fori_loop(jnp.where(early, chunks, 3), chunks, one, 0)
        for r in range(ROWS):
            heat_out(r).start()
        for r in range(-1, ROWS + 1):
            step_one(r)
            if r >= 1:
                step_two(r - 1, heat_s[r - 1])
        for r in range(ROWS):
            heat_out(r).wait()
        for r in range(ROWS):
            temp_out(r).wait()


def last(*arrays):
    whole = jax.ShapeDtypeStruct((LEV, ROWS, COLS), F32)
    track = pltpu.VMEM((ROWS, PAD, COLS), F32)
    return pl.pallas_call(
        last_kernel,
        out_shape=(whole, whole),
        in_specs=[VMEM] * 18,
        out_specs=(HBM, HBM),
        scratch_shapes=LIST_SCRATCH
        + [
            track,
            pltpu.VMEM((ROWS + 2, PAD, COLS), F32),
            track,
            pltpu.SemaphoreType.DMA((2,)),
        ],
        compiler_params=pltpu.CompilerParams(vmem_limit_bytes=32 << 20),
        cost_estimate=pl.CostEstimate(flops=10**10, bytes_accessed=8 * 10**6, transcendentals=0),
    )(*arrays)


def on_device(t, m, s, lit, k, w1, b1, w2, b2, w4, b4):
    lats, lons = lax.axis_size("lat"), lax.axis_size("lon")
    lit_row = jnp.concatenate([lit.reshape(1, ROWS), jnp.ones((1, COLS - ROWS), jnp.int32)], axis=1)
    t, m, *net, up, down, west, east = load(
        t, m, s, k, w1.T, b1.reshape(1, HID), w2, b2, w4, b4.reshape(1, LEV)
    )
    north = lax.ppermute(down, "lat", [(i, i + 1) for i in range(lats - 1)])
    south = lax.ppermute(up, "lat", [(i + 1, i) for i in range(lats - 1)])
    heat_a = some_rows(before_kernel, 2, lit_row, t, m, *net)
    west, east = corners(north, south, west, east)
    from_east = lax.ppermute(west, "lon", [(i, (i - 1) % lons) for i in range(lons)])
    from_west = lax.ppermute(east, "lon", [(i, (i + 1) % lons) for i in range(lons)])
    heat_b = some_rows(after_kernel, 3, lit_row, heat_a, t, m, *net)
    return last(lit_row, t, m, *net, heat_a, heat_b, north, south, west, east, from_west, from_east)


def solution(mesh):
    whole, plane = P(None, "lat", "lon"), P("lat", "lon")
    return jax.shard_map(
        on_device,
        mesh=mesh,
        in_specs=(whole, whole, plane, plane, plane) + (P(),) * 6,
        out_specs=(whole, whole),
        check_vma=False,
    )
```
